32 devices in a mesh: groups: 2 (over x), req: 8 (over z, y), head: 2 (over core).
Axes of the slice: x: 2, y: 2, z: 4, core: 2. Of those that a mesh axis runs over, the one named last changes fastest.
Arguments:
- queries: bfloat16 [2048, 32, 128], P(('groups', 'req'), 'head'), parts along dimension 0, may hold values from -100 to 100
- new_keys: bfloat16 [2048, 2, 128], P(('groups', 'req'), 'head'), parts along dimension 0, may hold values from -4.5 to 4.5
- new_values: bfloat16 [2048, 2, 128], P(('groups', 'req'), 'head'), parts along dimension 0, may hold values from -6 to 6
- cluster_kv: bfloat16 [1024, 2, 2, 128, 128], P(('groups', 'req'), 'head'), parts along dimension 0, may hold values from -6 to 6
- cluster_len: int32 [32], P('groups'), parts along dimension 0, may hold values from 1 to 4096, 40960 in all
- piece_slot: int32 [32, 32], P('groups'), parts along dimension 0, may hold values from 0 to 511, as said below
- cluster_ids: int32 [16, 2, 2], P('groups', 'head'), parts along dimension 0, may hold values from 0 to 15, all different within a row
- w_out: bfloat16 [4096, 4096], P('head', 'req'), may hold values from -0.09375 to 0.09375
Outputs:
- projected: bfloat16 [2048, 4096], P(('groups', 'req', 'head')), parts along dimension 0
The draws below stay inside these ranges and needn't reach their ends.
There are 2 independent parts, one for each index of `groups`. The reference program is written for one: setup_inputs(seed, part) draws one part's arguments, and reference() takes and returns one part's arrays. A program takes and returns all parts, laid end to end along the dimension named above; an argument that names none is the same for every part. Nothing has to cross between parts.
Inputs may be any that keep to these rules, and one draw needn't show every extreme that they name: `cluster_ids`: for each request and KV head, 2 distinct cluster numbers. A permutation of the slots: piece p of cluster c lies in slot piece_slot[c, p], stored on index slot // 64 of req, and every cluster has exactly 4 of its pieces on every index of req.
All inputs are finite; a program needn't handle non-finite values.
Results may differ from the reference program's by a relative error of at most 0.0052.
Values may be sent and summed in bfloat16 or wider, within the bound.
No kernel may reach another device: no remote copies, remote signals or barrier semaphores. Data moves between devices by JAX's collectives and lax.ppermute only.
A program may use at most 128 MiB of HBM per device.

```python
import math
import jax
import jax.numpy as jnp
import numpy as np
from jax import lax

D = 4096
HD = 128
QH = 32
KVH = 2
PIECE = 128
PCS = 32
NCL_DEV = 2
SEL = 2
TOK = 128
CL = 4096
NCL = 16
N_REQ = 8


def shared_keys(key):
    normal_keys = jax.random.normal(jax.random.fold_in(key, 7), (N_REQ * TOK, KVH, HD), jnp.float32)
    return jnp.clip(normal_keys, -4.5, 4.5)


def draw_new_keys(key, part):
    return shared_keys(key).astype(jnp.bfloat16)


def draw_queries(key, part):
    first_key = jax.random.fold_in(key, 13)
    second_key = jax.random.fold_in(key, 17)
    shape = (N_REQ * TOK, QH, HD)
    base = jax.random.normal(first_key, shape, jnp.float32)
    scales = jnp.exp(jax.random.uniform(second_key, (N_REQ * TOK, QH, 1), jnp.float32, -0.7, 1.1))
    result = base * scales
    return jnp.clip(result, -100.0, 100.0).astype(jnp.bfloat16)


def draw_piece_slot(key, part):
    per_peer = PCS // N_REQ
    held_slots = NCL_DEV * PCS
    first_scores = jax.random.randint(jax.random.fold_in(key, 41), (NCL, PCS), 0, 1 << 20) * PCS + jnp.arange(PCS, dtype=jnp.int32)[None, :]
    position = jnp.argsort(first_scores, axis=1).astype(jnp.int32)
    owner_index = position % N_REQ
    within = position // N_REQ
    second_scores = jax.random.randint(jax.random.fold_in(key, 42), (N_REQ, held_slots), 0, 1 << 20) * held_slots + jnp.arange(held_slots, dtype=jnp.int32)[None, :]
    device_perm = jnp.argsort(second_scores, axis=1).astype(jnp.int32)
    entry = jnp.arange(NCL, dtype=jnp.int32)[:, None] * per_peer + within
    local_slot = device_perm[owner_index, entry]
    return (owner_index * held_slots + local_slot).astype(jnp.int32)


def block_levels(key, extent, pieces, least, high):
    factor_of, own = 1.0, jax.random.fold_in(key, 6)
    for dim, parts in pieces:
        draws = jnp.exp(jax.random.uniform(jax.random.fold_in(own, dim), (parts,), jnp.float32, least / len(pieces), high / len(pieces)))
        factor_of = factor_of * jnp.repeat(draws, extent[dim] // parts).reshape([-1 if axis == dim else 1 for axis in range(len(extent))])
    return factor_of


def different_ones(stream_key, rows, count, top, lift):
    sequence = jax.random.permutation(jax.random.fold_in(stream_key, 1), count)
    boost = sequence
    for power in range(3):
        boost = boost * boost // count
    boost = boost * lift // count
    lots = jax.random.randint(jax.random.fold_in(stream_key, 2), (rows, count), 0, 4096) + boost
    fixed_rows = jax.random.permutation(jax.random.fold_in(stream_key, 3), rows)[jnp.arange(count) % rows]
    lots = jnp.where(jnp.arange(rows)[:, None] == fixed_rows[None, :], 1 << 14, lots)
    priority = lots * count + jnp.arange(count)
    return lax.top_k(priority.astype(jnp.int32), top)[1].astype(jnp.int32)


def length_profile(number_of, total, reach, skew):
    weights = [(1 << 20) // math.isqrt(standing ** skew) + 1 for standing in range(2, number_of + 1)]
    spare, counts = total - reach - (number_of - 1), [1] * (number_of - 1)
    while spare > 0:
        candidates = [i for i in range(number_of - 1) if counts[i] < reach]
        whole, remaining = sum([weights[i] for i in candidates]), spare
        for i in candidates:
            extra = min(reach - counts[i], max(1, remaining * weights[i] // whole), spare)
            counts[i] = counts[i] + extra
            spare = spare - extra
    return np.array([reach] + counts)


def ragged_sizes(key, count, total, limit, lean):
    if count == 2:
        one = jax.random.randint(key, (), max(1, total - limit), min(limit, total - 1) + 1)
        return jnp.stack([one, total - one])
    sizes = jnp.asarray(length_profile(count, total, limit, lean), jnp.int32)
    twos = (count - 1) // 2
    source_of, receiver = sizes[1:1 + 2 * twos:2], sizes[2:2 + 2 * twos:2]
    margin = jnp.minimum(source_of - 1, limit - receiver)
    passed = jax.random.randint(jax.random.fold_in(key, 1), (twos,), 0, 1 << 20) % (margin + 1)
    sizes = sizes.at[1:1 + 2 * twos:2].set(source_of - passed).at[2:2 + 2 * twos:2].set(receiver + passed)
    return sizes[jax.random.permutation(jax.random.fold_in(key, 2), count)]


def bell_draw(rng, extent, spread, reach, split=(), held_as=jnp.bfloat16):
    array = jax.random.normal(rng, extent, jnp.float32) * spread
    if len(split) > 0:
        array = block_levels(rng, extent, split, -0.22, 0.18) * array
    return jnp.clip(array, min=-reach, max=reach).astype(held_as)


def setup_inputs(seed: int = 0, part: int = 0) -> dict:
    streams_of = jax.random.split(jax.random.key(seed), 9)
    part_splits = jax.random.split(jax.random.fold_in(streams_of[8], part), 9)
    queries = draw_queries(jax.random.fold_in(jax.random.fold_in(streams_of[8], part), 71), part)
    new_keys = draw_new_keys(jax.random.fold_in(jax.random.fold_in(streams_of[8], part), 71), part)
    new_values = bell_draw(part_splits[2], (N_REQ * TOK, KVH, HD), 1.0, 6.0, ((0, 8), (1, 2)))
    cluster_kv = bell_draw(part_splits[3], (NCL * PCS, KVH, 2, PIECE, HD), 1.0, 6.0, ((0, 8), (1, 2)))
    cluster_len = ragged_sizes(part_splits[4], NCL, NCL * CL * 5 // 8, CL, 1).astype(jnp.int32)
    piece_slot = draw_piece_slot(jax.random.fold_in(jax.random.fold_in(streams_of[8], part), 71), part)
    cluster_ids = different_ones(part_splits[6], N_REQ * KVH, NCL, SEL, 1024).reshape((N_REQ, KVH, SEL))
    w_out = bell_draw(streams_of[7], (QH * HD, D), (QH * HD) ** -0.5, 0.09375, ((0, 2), (1, 8)))
    return {"queries": queries, "new_keys": new_keys, "new_values": new_values, "cluster_kv": cluster_kv, "cluster_len": cluster_len, "piece_slot": piece_slot, "cluster_ids": cluster_ids, "w_out": w_out}


def reference(queries, new_keys, new_values, cluster_kv, cluster_len, piece_slot, cluster_ids, w_out):
    group_size = QH // KVH
    scale_factor = HD ** -0.5
    position = jnp.arange(TOK, dtype=jnp.int32)
    causal = position[:, None] >= position[None, :]
    key_offset = (jnp.arange(PCS, dtype=jnp.int32)[:, None] * PIECE + jnp.arange(PIECE, dtype=jnp.int32)[None, :]).reshape(CL)

    def per_request(request):
        start_row = (request * TOK).astype(jnp.int32)
        query_rows = lax.dynamic_slice_in_dim(queries, start_row, TOK, 0)
        key_rows = lax.dynamic_slice_in_dim(new_keys, start_row, TOK, 0)
        value_rows = lax.dynamic_slice_in_dim(new_values, start_row, TOK, 0)
        plan_row = lax.dynamic_index_in_dim(cluster_ids, request, 0, keepdims=False)
        outputs = []
        for group_index in range(KVH):
            chosen = plan_row[group_index]
            slot_rows = piece_slot[chosen].reshape(SEL * PCS)
            picked = cluster_kv[slot_rows, group_index]
            lengths = cluster_len[chosen]
            valid_keys = (key_offset[None, :] < lengths[:, None]).reshape(SEL * CL)
            cached_keys = picked[:, 0].reshape(SEL * CL, HD).astype(jnp.float32)
            cached_values = picked[:, 1].reshape(SEL * CL, HD).astype(jnp.float32)
            own_keys = key_rows[:, group_index].astype(jnp.float32)
            own_values = value_rows[:, group_index].astype(jnp.float32)
            query_group = query_rows[:, group_index * group_size:(group_index + 1) * group_size].astype(jnp.float32)
            cached_scores = jnp.einsum("thd,kd->htk", query_group, cached_keys) * scale_factor
            cached_scores = jnp.where(valid_keys[None, None, :], cached_scores, -jnp.inf)
            own_scores = jnp.einsum("thd,ud->htu", query_group, own_keys) * scale_factor
            own_scores = jnp.where(causal[None], own_scores, -jnp.inf)
            row_top = jnp.maximum(jnp.max(cached_scores, axis=2), jnp.max(own_scores, axis=2))
            cached_weights = jnp.exp(cached_scores - row_top[:, :, None])
            own_weights = jnp.exp(own_scores - row_top[:, :, None])
            row_total = jnp.sum(cached_weights, axis=2) + jnp.sum(own_weights, axis=2)
            cached_low = cached_weights.astype(jnp.bfloat16).astype(jnp.float32)
            own_low = own_weights.astype(jnp.bfloat16).astype(jnp.float32)
            mixed_sum = jnp.einsum("htk,kd->htd", cached_low, cached_values) + jnp.einsum("htu,ud->htd", own_low, own_values)
            result = (mixed_sum / row_total[:, :, None]).astype(jnp.bfloat16)
            outputs.append(jnp.transpose(result, (1, 0, 2)))
        return jnp.concatenate(outputs, axis=1).reshape(TOK, QH * HD)

    attended = lax.map(per_request, jnp.arange(N_REQ, dtype=jnp.int32)).reshape(N_REQ * TOK, QH * HD)
    return jnp.dot(attended, w_out, preferred_element_type=jnp.float32).astype(jnp.bfloat16)
```

```python
import functools
import math

import jax
import jax.numpy as jnp
from jax import lax
from jax.experimental import pallas as pl
from jax.experimental.pallas import tpu as pltpu
from jax.sharding import PartitionSpec as P

LOW = -1e30
VMEM_LIMIT = 48 * 1024 * 1024


def swap(array, axis, size, mask):
    return lax.ppermute(array, axis, [(i, i ^ mask) for i in range(size)])


def pack_kernel(masks, partner, per_peer, slot_ref, ids_ref, kv_ref, *rest):
    outs, (table, sems) = rest[:-2], rest[-2:]
    me = lax.axis_index("req")
    clusters, pieces = slot_ref.shape
    held = kv_ref.shape[0]
    picks = ids_ref.shape[2]
    low = me * held

    def scan(c, carry):
        count = jnp.int32(0)
        for p in range(pieces):
            slot = slot_ref[c, p] - low
            table[c, count] = slot
            count = count + ((slot >= 0) & (slot < held)).astype(jnp.int32)
        return carry

    lax.fori_loop(0, clusters, scan, 0)
    copies = []
    for part in range(2):
        for index, mask in enumerate(masks):
            request = me ^ mask
            if part == 0:
                request = request ^ partner
            out = outs[part * len(masks) + index]
            for s in range(picks):
                c = ids_ref[request, 0, s]
                for k in range(per_peer):
                    copies.append(
                        pltpu.make_async_copy(
                            kv_ref.at[table[c, k], 0], out.at[s * per_peer + k], sems.at[len(copies)]
                        )
                    )
                    copies[-1].start()
    for copy in copies:
        copy.wait()


def pack(piece_slot, cluster_ids, cluster_kv, masks, partner, per_peer):
    picks = cluster_ids.shape[2]
    count = picks * per_peer
    shape = jax.ShapeDtypeStruct((count,) + cluster_kv.shape[2:], cluster_kv.dtype)
    smem = pl.BlockSpec(memory_space=pltpu.SMEM)
    anywhere = pl.BlockSpec(memory_space=pl.ANY)
    total = 2 * len(masks)
    size = total * count * math.prod(cluster_kv.shape[2:]) * 2
    return pl.pallas_call(
        functools.partial(pack_kernel, masks, partner, per_peer),
        out_shape=[shape] * total,
        in_specs=[smem, smem, anywhere],
        out_specs=[anywhere] * total,
        scratch_shapes=[
            pltpu.SMEM((piece_slot.shape[0], pieces_up(per_peer)), jnp.int32),
            pltpu.SemaphoreType.DMA((total * count,)),
        ],
        cost_estimate=pl.CostEstimate(flops=0, bytes_accessed=2 * size, transcendentals=0),
        name="pack_pieces",
    )(piece_slot, cluster_ids, cluster_kv)


def pieces_up(per_peer):
    return per_peer + 1


def attend_kernel(settings, *refs):
    own, heads, block, rows_step, picks, per_peer, sources, scale = settings
    if own:
        q_ref, valid_ref, slot_ref, pool_ref, own_k, own_v = refs[:6]
        rest = refs[6:]
    else:
        q_ref, valid_ref, slot_ref, pool_ref = refs[:4]
        rest = refs[4:]
    got = rest[: sources - 1]
    out_ref, stat_ref = rest[sources - 1 : sources + 1] if own else (rest[sources - 1], None)
    kv, bias, scores, tops, total, mixed, lse, sem = rest[sources + (1 if own else 0) :]
    rows, size = q_ref.shape
    keys = kv.shape[2]
    each = picks * per_peer
    lane = lax.broadcasted_iota(jnp.int32, (1, keys), 1)
    slots = kv.shape[0]

    at = jnp.int32(0)
    for j in range(sources):
        for e in range(each):
            valid = valid_ref[j, e]

            @pl.when(valid > 0)
            def _(j=j, e=e, valid=valid, at=at):
                source = pool_ref.at[slot_ref[e], 0] if j == 0 else got[j - 1].at[e]
                pltpu.make_async_copy(source, kv.at[at], sem).start()
                bias[at] = jnp.where(lane < valid, 0.0, LOW)

            at = at + (valid > 0).astype(jnp.int32)
    count = at
    blocks = (count + block - 1) // block

    @pl.when(count > 0)
    def _():
        for extra in range(block - 1):
            spot = count + extra

            @pl.when(spot < blocks * block)
            def _(spot=spot):
                pltpu.make_async_copy(pool_ref.at[0, 0], kv.at[spot], sem).start()
                bias[spot] = jnp.full((1, keys), LOW, jnp.float32)

    def wait(i, carry):
        pltpu.make_async_copy(pool_ref.at[0, 0], kv.at[0], sem).wait()
        return carry

    lax.fori_loop(0, blocks * block, wait, 0)

    def load(b, which):
        return kv[pl.ds(b * block, block), which].reshape(block * keys, size)

    def fold(values, op):
        parts = [values[:, i * keys : (i + 1) * keys] for i in range(values.shape[1] // keys)]
        while len(parts) > 1:
            parts = [op(parts[i], parts[i + 1]) if i + 1 < len(parts) else parts[i] for i in range(0, len(parts), 2)]
        return parts[0]

    def score(i, b):
        q = q_ref[pl.ds(i * rows_step, rows_step), :]
        s = lax.dot_general(q, load(b, 0), (((1,), (1,)), ((), ())), preferred_element_type=jnp.float32)
        line = bias[pl.ds(b * block, block)]
        s = s * scale + jnp.concatenate([line[n] for n in range(block)], axis=1)
        scores[i % 2, b] = s
        tops[i % 2] = jnp.maximum(tops[i % 2], fold(s, jnp.maximum))

    def start(i):
        if own:
            q = q_ref[pl.ds(i * rows_step, rows_step), :]
            s = lax.dot_general(q, own_k[...], (((1,), (1,)), ((), ())), preferred_element_type=jnp.float32)
            position = (lax.broadcasted_iota(jnp.int32, s.shape, 0) + i * rows_step) // heads
            s = jnp.where(position >= lax.broadcasted_iota(jnp.int32, s.shape, 1), s * scale, LOW)
            scores[i % 2, scores.shape[1] - 1, :, : s.shape[1]] = s
            tops[i % 2] = s
        else:
            tops[i % 2] = jnp.full(tops.shape[1:], LOW, jnp.float32)

    def weigh(i, b, top):
        p = jnp.exp2(scores[i % 2, b] - top)
        total[...] += fold(p, jnp.add)
        mixed[...] += jnp.dot(p.astype(jnp.bfloat16), load(b, 1), preferred_element_type=jnp.float32)

    steps = rows // rows_step
    eye = lax.broadcasted_iota(jnp.int32, (keys, keys), 0) == lax.broadcasted_iota(jnp.int32, (keys, keys), 1)
    for i in range(steps + 1):
        top = None
        if i > 0:
            top = jnp.max(tops[(i - 1) % 2], axis=1, keepdims=True)
            if own:
                p = jnp.exp2(scores[(i - 1) % 2, scores.shape[1] - 1, :, : own_k.shape[0]] - top)
                total[...] = p
                mixed[...] = jnp.dot(p.astype(jnp.bfloat16), own_v[...], preferred_element_type=jnp.float32)
            else:
                total[...] = jnp.zeros(total.shape, jnp.float32)
                mixed[...] = jnp.zeros(mixed.shape, jnp.float32)
        if i < steps:
            start(i)

        def body(b, carry, i=i, top=top):
            if i < steps:
                score(i, b)
            if i > 0:
                weigh(i - 1, b, top)
            return carry

        lax.fori_loop(0, blocks, body, 0)
        if i > 0:
            row_sum = jnp.sum(total[...], axis=1, keepdims=True)
            some = row_sum > 0.0
            safe = jnp.where(some, row_sum, 1.0)
            normal = mixed[...] / safe
            first = (i - 1) * rows_step
            out_ref[pl.ds(first, rows_step), :] = normal.astype(out_ref.dtype)
            log_sum = jnp.where(some, top + jnp.log2(safe), LOW)
            for n in range(rows_step // keys):
                column = log_sum[n * keys : (n + 1) * keys]
                line = jnp.sum(jnp.where(eye, column, 0.0), axis=0, keepdims=True)
                lse[pl.ds(first // keys + n, 1), :] = line
    if own:
        stat_ref[...] = lse[...]
    else:
        left = lse[...]
        lines = lse.shape[0]
        for n in range(3):
            part = left.astype(jnp.bfloat16)
            out_ref[pl.ds(rows + n * lines, lines), :] = part
            left = left - part.astype(jnp.float32)


def attend(q, valid, slots, pool, own_keys, own_values, got, heads):
    own = own_keys is not None
    rows, size = q.shape
    sources, each = valid.shape
    keys = pool.shape[3]
    block = 4
    rows_step = math.gcd(rows, 512)
    lines = rows // keys
    scale = size ** -0.5 * math.log2(math.e)
    picks = 1
    settings = (own, heads, block, rows_step, picks, each, sources, scale)
    smem = pl.BlockSpec(memory_space=pltpu.SMEM)
    vmem = pl.BlockSpec(memory_space=pltpu.VMEM)
    anywhere = pl.BlockSpec(memory_space=pl.ANY)
    most = -(-sources * each // block)
    if own:
        out_shape = [
            jax.ShapeDtypeStruct((rows, size), jnp.float32),
            jax.ShapeDtypeStruct((lines, keys), jnp.float32),
        ]
        operands = (q, valid, slots, pool, own_keys, own_values, *got)
        in_specs = [vmem, smem, smem, anywhere, vmem, vmem] + [anywhere] * len(got)
    else:
        out_shape = jax.ShapeDtypeStruct((rows + 3 * lines, size), jnp.bfloat16)
        operands = (q, valid, slots, pool, *got)
        in_specs = [vmem, smem, smem, anywhere] + [anywhere] * len(got)
    work = rows * sources * each * keys
    return pl.pallas_call(
        functools.partial(attend_kernel, settings),
        out_shape=out_shape,
        in_specs=in_specs,
        out_specs=[vmem, vmem] if own else vmem,
        scratch_shapes=[
            pltpu.VMEM((most * block,) + pool.shape[2:], pool.dtype),
            pltpu.VMEM((most * block, 1, keys), jnp.float32),
            pltpu.VMEM((2, most + (1 if own else 0), rows_step, block * keys), jnp.float32),
            pltpu.VMEM((2, rows_step, keys), jnp.float32),
            pltpu.VMEM((rows_step, keys), jnp.float32),
            pltpu.VMEM((rows_step, size), jnp.float32),
            pltpu.VMEM((lines, keys), jnp.float32),
            pltpu.SemaphoreType.DMA,
        ],
        compiler_params=pltpu.CompilerParams(vmem_limit_bytes=VMEM_LIMIT),
        cost_estimate=pl.CostEstimate(flops=8 * work * size, bytes_accessed=4 << 20, transcendentals=work),
        name="attend_own" if own else "attend_partner",
    )(*operands)


def combine_kernel(heads, out_mine, lse_mine, other, attended, scratch):
    rows, size = out_mine.shape
    lines, keys = lse_mine.shape
    eye = lax.broadcasted_iota(jnp.int32, (keys, keys), 0) == lax.broadcasted_iota(jnp.int32, (keys, keys), 1)
    mine = lse_mine[...]
    theirs = sum(other[pl.ds(rows + n * lines, lines), :].astype(jnp.float32) for n in range(3))
    top = jnp.maximum(mine, theirs)
    mine, theirs = jnp.exp2(mine - top), jnp.exp2(theirs - top)
    share = theirs / (mine + theirs)
    for n in range(lines):
        column = jnp.sum(jnp.where(eye, share[n : n + 1], 0.0), axis=1, keepdims=True)
        here = pl.ds(n * keys, keys)
        a = out_mine[here, :]
        scratch[here, :] = a + column * (other[here, :].astype(jnp.float32) - a)
    tokens = rows // heads
    for h in range(heads):
        attended[:, h * size : (h + 1) * size] = scratch[pl.ds(h, tokens, stride=heads), :].astype(attended.dtype)


def combine(out_mine, lse_mine, other, heads):
    rows, size = out_mine.shape
    vmem = pl.BlockSpec(memory_space=pltpu.VMEM)
    return pl.pallas_call(
        functools.partial(combine_kernel, heads),
        out_shape=jax.ShapeDtypeStruct((rows // heads, heads * size), jnp.bfloat16),
        in_specs=[vmem] * 3,
        out_specs=vmem,
        scratch_shapes=[pltpu.VMEM((rows, size), jnp.float32)],
        compiler_params=pltpu.CompilerParams(vmem_limit_bytes=VMEM_LIMIT),
        cost_estimate=pl.CostEstimate(flops=4 * rows * size, bytes_accessed=8 * rows * size, transcendentals=0),
        name="combine",
    )(out_mine, lse_mine, other)


def place_kernel(masks, *refs):
    parts, (out, sems) = refs[:-2], refs[-2:]
    me = lax.axis_index("req")
    width = parts[0].shape[2]
    copies = []
    for part, mask in zip(parts, masks):
        for side in range(2):
            column = ((me ^ mask) ^ side) * width
            copies.append(
                pltpu.make_async_copy(
                    part.at[side], out.at[:, pl.ds(pl.multiple_of(column, 128), width)], sems.at[len(copies)]
                )
            )
            copies[-1].start()
    for copy in copies:
        copy.wait()


def place(parts, masks):
    _, rows, width = parts[0].shape
    anywhere = pl.BlockSpec(memory_space=pl.ANY)
    return pl.pallas_call(
        functools.partial(place_kernel, masks),
        out_shape=jax.ShapeDtypeStruct((rows, 2 * len(parts) * width), parts[0].dtype),
        in_specs=[anywhere] * len(parts),
        out_specs=anywhere,
        scratch_shapes=[pltpu.SemaphoreType.DMA((2 * len(parts),))],
        name="place_columns",
    )(*parts)


def local(queries, new_keys, new_values, cluster_kv, cluster_len, piece_slot, cluster_ids, w_out):
    me = lax.axis_index("req")
    core = lax.axis_index("head")
    peers = lax.axis_size("req")
    cores = lax.axis_size("head")
    tokens, heads, size = queries.shape
    held = cluster_kv.shape[0]
    keys = cluster_kv.shape[3]
    pieces = piece_slot.shape[1]
    per_peer = pieces // peers
    half = peers // 2
    masks = list(range(1, half))

    packed = pack(piece_slot, cluster_ids, cluster_kv, masks, half, per_peer)
    q_mine = queries.reshape(tokens * heads, size)
    q_theirs = swap(q_mine, "req", peers, half)
    got_theirs = [swap(a, "req", peers, m) for a, m in zip(packed[: len(masks)], masks)]

    owner = piece_slot // held
    position = jnp.arange(pieces, dtype=jnp.int32)
    same = (owner[:, :, None] == owner[:, None, :]) & (position[:, None] > position[None, :])[None]
    rank = jnp.sum(same.astype(jnp.int32), axis=2)

    def tables(request):
        chosen = lax.dynamic_index_in_dim(cluster_ids, request, 0, keepdims=False)[0]
        own_owner, own_rank, own_slot = owner[chosen], rank[chosen], piece_slot[chosen] % held
        sender = me ^ jnp.arange(half, dtype=jnp.int32)
        fits = (own_owner[None, :, None, :] == sender[:, None, None, None]) & (
            own_rank[None, :, None, :] == jnp.arange(per_peer, dtype=jnp.int32)[None, None, :, None]
        )
        filled = jnp.clip(cluster_len[chosen][:, None] - position[None, :] * keys, 0, keys)
        valid = jnp.sum(jnp.where(fits, filled[None, :, None, :], 0), axis=3).reshape(half, -1)
        slots = jnp.sum(jnp.where(fits[0], own_slot[:, None, :], 0), axis=2).reshape(-1)
        return valid, slots

    valid_theirs, slots_theirs = tables(me ^ half)
    valid_mine, slots_mine = tables(me)

    part = attend(q_theirs, valid_theirs, slots_theirs, cluster_kv, None, None, got_theirs, heads)
    later = lax.optimization_barrier((tuple(packed[len(masks) :]), tuple(got_theirs)))[0]
    got_mine = [swap(a, "req", peers, m) for a, m in zip(later, masks)]
    part = swap(part, "req", peers, half)
    w_later = lax.optimization_barrier((w_out, tuple(got_mine)))[0]
    w_pair = swap(w_later, "req", peers, 1)
    mine, lse = attend(
        q_mine, valid_mine, slots_mine, cluster_kv, new_keys[:, 0], new_values[:, 0], got_mine, heads
    )
    attended = combine(mine, lse, part, heads)

    have = {0: attended}
    bit = half
    while bit > 1:
        for mask in list(have):
            have[mask ^ bit] = swap(have[mask], "req", peers, bit)
        bit //= 2

    share = tokens // cores
    results = {}
    for mask, rows in have.items():
        def product(which, rows=rows):
            few = lax.dynamic_slice_in_dim(rows, which * share, share, 0)
            return [jnp.dot(few, w, preferred_element_type=jnp.float32) for w in (w_out, w_pair)]

        away = jnp.stack([a.astype(jnp.bfloat16) for a in product(core ^ 1)])
        away = swap(away, "head", cores, 1)
        summed = (jnp.stack(product(core)) + away.astype(jnp.float32)).astype(jnp.bfloat16)
        results[mask] = swap(summed, "req", peers, mask) if mask else summed
    return place(list(results.values()), list(results))


def solution(mesh):
    return jax.shard_map(
        local,
        mesh=mesh,
        in_specs=(
            P(("groups", "req"), "head", None),
            P(("groups", "req"), "head", None),
            P(("groups", "req"), "head", None),
            P(("groups", "req"), "head", None, None, None),
            P("groups"),
            P("groups", None),
            P("groups", "head", None),
            P("head", "req"),
        ),
        out_specs=P(("groups", "req", "head"), None),
        check_vma=False,
    )
```

```python
import functools
import math

import jax
import jax.numpy as jnp
from jax import lax
from jax.experimental import pallas as pl
from jax.experimental.pallas import tpu as pltpu
from jax.sharding import PartitionSpec as P

LOW = -1e30
VMEM_LIMIT = 48 * 1024 * 1024


def swap(array, axis, size, mask):
    return lax.ppermute(array, axis, [(i, i ^ mask) for i in range(size)])


def pack_kernel(masks, partner, per_peer, slot_ref, ids_ref, kv_ref, *rest):
    outs, (table, sems) = rest[:-2], rest[-2:]
    me = lax.axis_index("req")
    clusters, pieces = slot_ref.shape
    held = kv_ref.shape[0]
    picks = ids_ref.shape[0]
    low = me * held

    def scan(c, carry):
        count = jnp.int32(0)
        for p in range(pieces):
            slot = slot_ref[c, p] - low
            table[c, count] = slot
            count = count + ((slot >= 0) & (slot < held)).astype(jnp.int32)
        return carry

    lax.fori_loop(0, clusters, scan, 0)
    copies = []
    for part in range(2):
        for index, mask in enumerate(masks):
            request = me ^ mask
            if part == 0:
                request = request ^ partner
            out = outs[part * len(masks) + index]
            for s in range(picks):
                c = ids_ref[s, request]
                for k in range(per_peer):
                    copies.append(
                        pltpu.make_async_copy(
                            kv_ref.at[table[c, k], 0], out.at[s * per_peer + k], sems.at[len(copies)]
                        )
                    )
                    copies[-1].start()
    for copy in copies:
        copy.wait()


def pack(piece_slot, plan, cluster_kv, masks, partner, per_peer):
    count = plan.shape[0] * per_peer
    shape = jax.ShapeDtypeStruct((count,) + cluster_kv.shape[2:], cluster_kv.dtype)
    smem = pl.BlockSpec(memory_space=pltpu.SMEM)
    total = 2 * len(masks)
    size = total * count * math.prod(cluster_kv.shape[2:]) * 2
    return pl.pallas_call(
        functools.partial(pack_kernel, masks, partner, per_peer),
        out_shape=[shape] * total,
        in_specs=[smem, smem, pl.BlockSpec(memory_space=pl.ANY)],
        out_specs=[pl.BlockSpec(memory_space=pltpu.VMEM)] * total,
        scratch_shapes=[
            pltpu.SMEM((piece_slot.shape[0], per_peer + 1), jnp.int32),
            pltpu.SemaphoreType.DMA((total * count,)),
        ],
        compiler_params=pltpu.CompilerParams(vmem_limit_bytes=VMEM_LIMIT),
        cost_estimate=pl.CostEstimate(flops=0, bytes_accessed=2 * size, transcendentals=0),
        name="pack_pieces",
    )(piece_slot, plan, cluster_kv)


def attend_kernel(settings, *refs):
    own, heads, block, rows_step, sources, scale, mode, earlier, packed = settings
    refs = list(refs)

    def take(n):
        taken, refs[:] = refs[:n], refs[n:]
        return taken

    q_ref, valid_ref = take(2)
    slot_ref, pool_ref = take(2) if 0 in sources else (None, None)
    own_k, own_v = take(2) if own else (None, None)
    got = dict(zip([j for j in sources if j], take(len([j for j in sources if j]))))
    before = take(2) if earlier else None
    other = take(1)[0] if packed else None
    outs = take(2 if mode == "state" else 1)
    kv, bias, scores, tops, total, mixed, lse, sem = refs
    rows, size = q_ref.shape
    keys = kv.shape[2]
    each = valid_ref.shape[1]
    lane = lax.broadcasted_iota(jnp.int32, (1, keys), 1)
    lines = rows // keys

    def piece(j, e):
        return got[j].at[e] if j else pool_ref.at[slot_ref[e], 0]

    at = jnp.int32(0)
    for j in sources:
        for e in range(each):
            valid = valid_ref[j, e]

            @pl.when(valid > 0)
            def _(j=j, e=e, valid=valid, at=at):
                pltpu.make_async_copy(piece(j, e), kv.at[at], sem).start()
                bias[at] = jnp.where(lane < valid, 0.0, LOW)

            at = at + (valid > 0).astype(jnp.int32)
    count = at
    blocks = (count + block - 1) // block
    for extra in range(block - 1):
        spot = count + extra

        @pl.when(spot < blocks * block)
        def _(spot=spot):
            pltpu.make_async_copy(piece(sources[0], 0), kv.at[spot], sem).start()
            bias[spot] = jnp.full((1, keys), LOW, jnp.float32)

    def wait(i, carry):
        pltpu.make_async_copy(piece(sources[0], 0), kv.at[0], sem).wait()
        return carry

    lax.fori_loop(0, blocks * block, wait, 0)

    def load(b, which):
        return kv[pl.ds(b * block, block), which].reshape(block * keys, size)

    def fold(values, op):
        parts = [values[:, i * keys : (i + 1) * keys] for i in range(values.shape[1] // keys)]
        while len(parts) > 1:
            parts = [op(parts[i], parts[i + 1]) if i + 1 < len(parts) else parts[i] for i in range(0, len(parts), 2)]
        return parts[0]

    def score(i, b):
        q = q_ref[pl.ds(i * rows_step, rows_step), :]
        s = lax.dot_general(q, load(b, 0), (((1,), (1,)), ((), ())), preferred_element_type=jnp.float32)
        line = bias[pl.ds(b * block, block)]
        s = s * scale + jnp.concatenate([line[n] for n in range(block)], axis=1)
        scores[i % 2, b] = s
        tops[i % 2] = jnp.maximum(tops[i % 2], fold(s, jnp.maximum))

    def start(i):
        if own:
            q = q_ref[pl.ds(i * rows_step, rows_step), :]
            s = lax.dot_general(q, own_k[...], (((1,), (1,)), ((), ())), preferred_element_type=jnp.float32)
            position = (lax.broadcasted_iota(jnp.int32, s.shape, 0) + i * rows_step) // heads
            s = jnp.where(position >= lax.broadcasted_iota(jnp.int32, s.shape, 1), s * scale, LOW)
            scores[i % 2, scores.shape[1] - 1, :, : s.shape[1]] = s
            tops[i % 2] = fold(s, jnp.maximum)
        else:
            tops[i % 2] = jnp.full(tops.shape[1:], LOW, jnp.float32)

    def weigh(i, b, top):
        p = jnp.exp2(scores[i % 2, b] - top)
        total[...] += fold(p, jnp.add)
        mixed[...] += jnp.dot(p.astype(jnp.bfloat16), load(b, 1), preferred_element_type=jnp.float32)

    steps = rows // rows_step
    group = rows_step // keys
    eye = lax.broadcasted_iota(jnp.int32, (keys, keys), 0) == lax.broadcasted_iota(jnp.int32, (keys, keys), 1)

    def finish(i, top):
        row_sum = jnp.sum(total[...], axis=1, keepdims=True)
        some = row_sum > 0.0
        safe = jnp.where(some, row_sum, 1.0)
        normal = mixed[...] / safe
        first = i * rows_step
        here = pl.ds(first, rows_step)
        column = jnp.where(some, top + jnp.log2(safe), LOW)
        mine = jnp.concatenate(
            [
                jnp.sum(jnp.where(eye, column[n * keys : (n + 1) * keys], 0.0), axis=0, keepdims=True)
                for n in range(group)
            ],
            axis=0,
        )
        spots = pl.ds(i * group, group)
        rest = []
        if earlier:
            rest.append((before[0][here, :], before[1][spots, :]))
        if packed:
            logs = other[pl.ds(rows, 3 * lines), :].astype(jnp.float32)
            logs = sum(logs[n * lines + i * group : n * lines + (i + 1) * group] for n in range(3))
            rest.append((other[here, :].astype(jnp.float32), logs))
        if rest:
            peak = functools.reduce(jnp.maximum, [logs for _, logs in rest], mine)
            powers = [jnp.exp2(logs - peak) for _, logs in rest]
            whole = sum(powers, jnp.exp2(mine - peak))
            mine = peak + jnp.log2(whole)
            result = normal
            for (values, _), power in zip(rest, powers):
                share = power / whole
                wide = jnp.concatenate(
                    [
                        jnp.sum(jnp.where(eye, share[n : n + 1], 0.0), axis=1, keepdims=True)
                        for n in range(group)
                    ],
                    axis=0,
                )
                result = result + wide * (values - normal)
            normal = result
        if mode == "state":
            outs[0][here, :] = normal
            outs[1][spots, :] = mine
        elif mode == "packed":
            outs[0][here, :] = normal.astype(jnp.bfloat16)
            lse[spots, :] = mine
        else:
            mixed[...] = normal
            tokens = rows_step // heads
            for h in range(heads):
                outs[0][pl.ds(i * tokens, tokens), h * size : (h + 1) * size] = mixed[
                    pl.ds(h, tokens, stride=heads), :
                ].astype(jnp.bfloat16)

    for i in range(steps + 1):
        top = None
        if i > 0:
            top = jnp.max(tops[(i - 1) % 2], axis=1, keepdims=True)
            if own:
                p = jnp.exp2(scores[(i - 1) % 2, scores.shape[1] - 1, :, : own_k.shape[0]] - top)
                total[...] = fold(p, jnp.add)
                mixed[...] = jnp.dot(p.astype(jnp.bfloat16), own_v[...], preferred_element_type=jnp.float32)
            else:
                total[...] = jnp.zeros(total.shape, jnp.float32)
                mixed[...] = jnp.zeros(mixed.shape, jnp.float32)
        if i < steps:
            start(i)

        def body(b, carry, i=i, top=top):
            if i < steps:
                score(i, b)
            if i > 0:
                weigh(i - 1, b, top)
            return carry

        lax.fori_loop(0, blocks, body, 0)
        if i > 0:
            finish(i - 1, top)
    if mode == "packed":
        left = lse[...]
        for n in range(3):
            part = left.astype(jnp.bfloat16)
            outs[0][pl.ds(rows + n * lines, lines), :] = part
            left = left - part.astype(jnp.float32)


def attend(name, mode, heads, q, valid, got, local=None, own=None, earlier=None, packed=None):
    rows, size = q.shape
    each = valid.shape[1]
    sources = ([0] if local is not None else []) + list(got)
    keys = size
    block = 4
    rows_step = math.gcd(rows, 512)
    lines = rows // keys
    scale = size ** -0.5 * math.log2(math.e)
    settings = (
        own is not None, heads, block, rows_step, sources, scale, mode, earlier is not None, packed is not None
    )
    smem = pl.BlockSpec(memory_space=pltpu.SMEM)
    vmem = pl.BlockSpec(memory_space=pltpu.VMEM)
    anywhere = pl.BlockSpec(memory_space=pl.ANY)
    operands, in_specs = [q, valid], [vmem, smem]
    if local is not None:
        operands, in_specs = operands + list(local), in_specs + [smem, anywhere]
    if own is not None:
        operands, in_specs = operands + list(own), in_specs + [vmem] * 2
    operands, in_specs = operands + list(got.values()), in_specs + [anywhere] * len(got)
    if earlier is not None:
        operands, in_specs = operands + list(earlier), in_specs + [vmem] * 2
    if packed is not None:
        operands, in_specs = operands + [packed], in_specs + [vmem]
    if mode == "state":
        out_shape = [
            jax.ShapeDtypeStruct((rows, size), jnp.float32),
            jax.ShapeDtypeStruct((lines, keys), jnp.float32),
        ]
    elif mode == "packed":
        out_shape = [jax.ShapeDtypeStruct((rows + 3 * lines, size), jnp.bfloat16)]
    else:
        out_shape = [jax.ShapeDtypeStruct((rows // heads, heads * size), jnp.bfloat16)]
    most = -(-len(sources) * each // block)
    shape = (2, keys, size)
    work = rows * len(sources) * each * keys
    out = pl.pallas_call(
        functools.partial(attend_kernel, settings),
        out_shape=out_shape,
        in_specs=in_specs,
        out_specs=[vmem] * len(out_shape),
        scratch_shapes=[
            pltpu.VMEM((most * block,) + shape, q.dtype),
            pltpu.VMEM((most * block, 1, keys), jnp.float32),
            pltpu.VMEM((2, most + (1 if own is not None else 0), rows_step, block * keys), jnp.float32),
            pltpu.VMEM((2, rows_step, keys), jnp.float32),
            pltpu.VMEM((rows_step, keys), jnp.float32),
            pltpu.VMEM((rows_step, size), jnp.float32),
            pltpu.VMEM((lines, keys), jnp.float32),
            pltpu.SemaphoreType.DMA,
        ],
        compiler_params=pltpu.CompilerParams(vmem_limit_bytes=VMEM_LIMIT),
        cost_estimate=pl.CostEstimate(flops=8 * work * size, bytes_accessed=4 << 20, transcendentals=work),
        name=name,
    )(*operands)
    return out if mode == "state" else out[0]


def project_kernel(attended, w_mine, w_pair, away, keep, scratch):
    core = lax.axis_index("head")
    share = away.shape[1]
    for side, w in enumerate((w_mine, w_pair)):
        scratch[side] = jnp.dot(attended[...], w[...], preferred_element_type=jnp.float32)
        away[side] = scratch[side, pl.ds(pl.multiple_of((core ^ 1) * share, share), share), :].astype(jnp.bfloat16)
        keep[side] = scratch[side, pl.ds(pl.multiple_of(core * share, share), share), :]


def project(attended, w_mine, w_pair, cores):
    tokens, depth = attended.shape
    width = w_mine.shape[1]
    share = tokens // cores
    vmem = pl.BlockSpec(memory_space=pltpu.VMEM)
    return pl.pallas_call(
        project_kernel,
        out_shape=[
            jax.ShapeDtypeStruct((2, share, width), jnp.bfloat16),
            jax.ShapeDtypeStruct((2, share, width), jnp.float32),
        ],
        in_specs=[vmem] * 3,
        out_specs=[vmem] * 2,
        scratch_shapes=[pltpu.VMEM((2, tokens, width), jnp.float32)],
        compiler_params=pltpu.CompilerParams(vmem_limit_bytes=VMEM_LIMIT),
        cost_estimate=pl.CostEstimate(
            flops=4 * tokens * depth * width, bytes_accessed=4 * depth * width, transcendentals=0
        ),
        name="project",
    )(attended, w_mine, w_pair)


def place_kernel(masks, *refs):
    parts, out = refs[:-1], refs[-1]
    me = lax.axis_index("req")
    width = parts[0].shape[2]
    for part, mask in zip(parts, masks):
        for side in range(2):
            column = ((me ^ mask) ^ side) * width
            out[:, pl.ds(pl.multiple_of(column, width), width)] = part[side]


def place(parts, masks):
    _, rows, width = parts[0].shape
    vmem = pl.BlockSpec(memory_space=pltpu.VMEM)
    return pl.pallas_call(
        functools.partial(place_kernel, masks),
        out_shape=jax.ShapeDtypeStruct((rows, 2 * len(parts) * width), parts[0].dtype),
        in_specs=[vmem] * len(parts),
        out_specs=vmem,
        compiler_params=pltpu.CompilerParams(vmem_limit_bytes=VMEM_LIMIT),
        name="place_columns",
    )(*parts)


def local(queries, new_keys, new_values, cluster_kv, cluster_len, piece_slot, cluster_ids, w_out):
    me = lax.axis_index("req")
    core = lax.axis_index("head")
    peers = lax.axis_size("req")
    cores = lax.axis_size("head")
    tokens, heads, size = queries.shape
    held = cluster_kv.shape[0]
    keys = cluster_kv.shape[3]
    pieces = piece_slot.shape[1]
    per_peer = pieces // peers
    half = peers // 2
    masks = list(range(1, half))

    plan = cluster_ids[:, 0]
    packed = pack(piece_slot, plan.T, cluster_kv, masks, half, per_peer)
    q_mine = queries.reshape(tokens * heads, size)
    q_theirs = swap(q_mine, "req", peers, half)
    got_theirs = [swap(a, "req", peers, m) for a, m in zip(packed[: len(masks)], masks)]

    owner = piece_slot // held
    position = jnp.arange(pieces, dtype=jnp.int32)
    same = (owner[:, :, None] == owner[:, None, :]) & (position[:, None] > position[None, :])[None]
    rank = jnp.sum(same.astype(jnp.int32), axis=2)

    def tables(request):
        chosen = lax.dynamic_index_in_dim(plan, request, 0, keepdims=False)
        own_owner, own_rank, own_slot = owner[chosen], rank[chosen], piece_slot[chosen] % held
        sender = me ^ jnp.arange(half, dtype=jnp.int32)
        fits = (own_owner[None, :, None, :] == sender[:, None, None, None]) & (
            own_rank[None, :, None, :] == jnp.arange(per_peer, dtype=jnp.int32)[None, None, :, None]
        )
        filled = jnp.clip(cluster_len[chosen][:, None] - position[None, :] * keys, 0, keys)
        valid = jnp.sum(jnp.where(fits, filled[None, :, None, :], 0), axis=3).reshape(half, -1)
        slots = jnp.sum(jnp.where(fits[0], own_slot[:, None, :], 0), axis=2).reshape(-1)
        return valid, slots

    valid_theirs, slots_theirs = tables(me ^ half)
    valid_mine, slots_mine = tables(me)

    got = dict(zip(masks, got_theirs))
    last, late = masks[-1:], masks[-2:-1]
    early = [m for m in masks if m not in last + late]

    def some(chosen):
        return {m: got[m] for m in chosen}

    state = attend(
        "attend_partner_early", "state", heads, q_theirs, valid_theirs, some(early), (slots_theirs, cluster_kv)
    )
    state = attend("attend_partner_late", "state", heads, q_theirs, valid_theirs, some(late), earlier=state)
    part = attend("attend_partner_last", "packed", heads, q_theirs, valid_theirs, some(last), earlier=state)

    later = lax.optimization_barrier((tuple(packed[len(masks) :]), tuple(got_theirs)))[0]
    got_mine = [swap(a, "req", peers, m) for a, m in zip(later, masks)]
    got = dict(zip(masks, got_mine))
    part = swap(part, "req", peers, half)
    w_later = lax.optimization_barrier((w_out, tuple(got_mine)))[0]
    w_pair = swap(w_later, "req", peers, 1)
    state = attend(
        "attend_own_local", "state", heads, q_mine, valid_mine, {}, (slots_mine, cluster_kv),
        (new_keys[:, 0], new_values[:, 0]),
    )
    if early:
        state = attend("attend_own_early", "state", heads, q_mine, valid_mine, some(early), earlier=state)
    state = attend("attend_own_late", "state", heads, q_mine, valid_mine, some(late), earlier=state)
    attended = attend(
        "attend_own_last", "final", heads, q_mine, valid_mine, some(last), earlier=state, packed=part
    )

    have = {0: attended}
    bit = half
    while bit > 1:
        for mask in list(have):
            have[mask ^ bit] = swap(have[mask], "req", peers, bit)
        bit //= 2

    results = {}
    for mask, rows in have.items():
        away, keep = project(rows, w_out, w_pair, cores)
        away = swap(away, "head", cores, 1)
        summed = (keep + away.astype(jnp.float32)).astype(jnp.bfloat16)
        results[mask] = swap(summed, "req", peers, mask) if mask else summed
    return place(list(results.values()), list(results))


def solution(mesh):
    return jax.shard_map(
        local,
        mesh=mesh,
        in_specs=(
            P(("groups", "req"), "head", None),
            P(("groups", "req"), "head", None),
            P(("groups", "req"), "head", None),
            P(("groups", "req"), "head", None, None, None),
            P("groups"),
            P("groups", None),
            P("groups", "head", None),
            P("head", "req"),
        ),
        out_specs=P(("groups", "req", "head"), None),
        check_vma=False,
    )
```

```python
import functools
import math

import jax
import jax.numpy as jnp
from jax import lax
from jax.experimental import pallas as pl
from jax.experimental.pallas import tpu as pltpu
from jax.sharding import PartitionSpec as P

LOW = -1e30
VMEM_SMALL = 16 * 1024 * 1024
VMEM_MOST = 60 * 1024 * 1024
COST = pl.CostEstimate(flops=1024, bytes_accessed=1024, transcendentals=0)
SHORT = pl.CostEstimate(flops=1 << 31, bytes_accessed=1024, transcendentals=0)
LONG = pl.CostEstimate(flops=1 << 40, bytes_accessed=1024, transcendentals=0)


def swap(array, axis, size, mask):
    return lax.ppermute(array, axis, [(i, i ^ mask) for i in range(size)])


def pack_kernel(wanted, per_peer, slot_ref, ids_ref, kv_ref, *rest):
    outs, (slots, ids, table, sems, first) = rest[:-5], rest[-5:]
    loads = [
        pltpu.make_async_copy(slot_ref, slots, first.at[0]),
        pltpu.make_async_copy(ids_ref, ids, first.at[1]),
    ]
    for copy in loads:
        copy.start()
    for copy in loads:
        copy.wait()
    me = lax.axis_index("req")
    pieces = slots.shape[1]
    held = kv_ref.shape[0]
    picks = ids.shape[0]
    low = me * held
    copies = []
    for out, mask in zip(outs, wanted):
        for s in range(picks):
            row = (len(copies) // per_peer) % table.shape[0]
            c = ids[s, me ^ mask]

            def scan(p, count, c=c, row=row):
                slot = slots[c, p] - low
                table[row, count] = slot
                return count + ((slot >= 0) & (slot < held)).astype(jnp.int32)

            lax.fori_loop(0, pieces, scan, jnp.int32(0), unroll=8)
            for k in range(per_peer):
                copies.append(
                    pltpu.make_async_copy(kv_ref.at[table[row, k], 0], out.at[s * per_peer + k], sems.at[len(copies)])
                )
                copies[-1].start()
    for copy in copies:
        copy.wait()


def pack(piece_slot, plan, cluster_kv, wanted, per_peer):
    count = plan.shape[0] * per_peer
    shape = jax.ShapeDtypeStruct((count,) + cluster_kv.shape[2:], cluster_kv.dtype)
    hbm = pl.BlockSpec(memory_space=pltpu.HBM)
    total = len(wanted)
    return pl.pallas_call(
        functools.partial(pack_kernel, wanted, per_peer),
        out_shape=[shape] * total,
        in_specs=[hbm] * 3,
        out_specs=[pl.BlockSpec(memory_space=pltpu.VMEM)] * total,
        scratch_shapes=[
            pltpu.SMEM(piece_slot.shape, jnp.int32),
            pltpu.SMEM(plan.shape, jnp.int32),
            pltpu.SMEM((total * plan.shape[0], per_peer + 1), jnp.int32),
            pltpu.SemaphoreType.DMA((total * count,)),
            pltpu.SemaphoreType.DMA((2,)),
        ],
        compiler_params=pltpu.CompilerParams(vmem_limit_bytes=VMEM_MOST),
        cost_estimate=COST,
        name="pack_pieces",
    )(piece_slot, plan, cluster_kv)


def fold(values, keys, op):
    parts = [values[:, i * keys : (i + 1) * keys] for i in range(values.shape[1] // keys)]
    while len(parts) > 1:
        parts = [op(parts[i], parts[i + 1]) if i + 1 < len(parts) else parts[i] for i in range(0, len(parts), 2)]
    return parts[0]


def to_lines(column, eye):
    keys = eye.shape[0]
    return jnp.concatenate(
        [
            jnp.sum(jnp.where(eye, column[n : n + keys], 0.0), axis=0, keepdims=True)
            for n in range(0, column.shape[0], keys)
        ],
        axis=0,
    )


def to_column(lines, eye):
    return jnp.concatenate(
        [jnp.sum(jnp.where(eye, lines[n : n + 1], 0.0), axis=1, keepdims=True) for n in range(lines.shape[0])],
        axis=0,
    )


def diagonal(keys):
    return lax.broadcasted_iota(jnp.int32, (keys, keys), 0) == lax.broadcasted_iota(jnp.int32, (keys, keys), 1)


def attend_kernel(settings, *refs):
    own, heads, rows_step, sources, scale, mode, earlier = settings
    refs = list(refs)

    def take(n):
        taken, refs[:] = refs[:n], refs[n:]
        return taken

    q_ref, valid_ref = take(2)
    own_k, own_v = take(2) if own else (None, None)
    got = take(len(sources))
    before = take(2) if earlier else None
    outs = take(2)
    scores, own_scores, mixed, lse = refs
    rows, size = q_ref.shape
    each, _, keys, _ = got[0].shape
    lines = rows // keys
    group = rows_step // keys
    lane = lax.broadcasted_iota(jnp.int32, (1, keys), 1)
    eye = diagonal(keys)
    biases, any_valid = [], jnp.int32(0)
    for j in sources:
        valid = [valid_ref[j, e] for e in range(each)]
        biases.append(jnp.concatenate([jnp.where(lane < v, 0.0, LOW) for v in valid], axis=1))
        any_valid = sum(valid, any_valid)

    def dot_t(x, y):
        return lax.dot_general(x, y, (((1,), (1,)), ((), ())), preferred_element_type=jnp.float32)

    for i in range(rows // rows_step):
        here = pl.ds(i * rows_step, rows_step)
        spots = pl.ds(i * group, group)
        q = q_ref[here, :]
        tops = []
        if own:
            s = dot_t(q, own_k[...])
            position = (lax.broadcasted_iota(jnp.int32, s.shape, 0) + i * rows_step) // heads
            s = jnp.where(position >= lax.broadcasted_iota(jnp.int32, s.shape, 1), s * scale, LOW)
            own_scores[i % 2] = s
            tops.append(s)
        for b, pieces in enumerate(got):
            s = dot_t(q, pieces[:, 0].reshape(each * keys, size)) * scale + biases[b]
            scores[i % 2, b] = s
            tops.append(fold(s, keys, jnp.maximum))
        top = jnp.max(functools.reduce(jnp.maximum, tops), axis=1, keepdims=True)
        total, mix = [], []
        if own:
            p = jnp.exp2(own_scores[i % 2] - top)
            total.append(fold(p, keys, jnp.add))
            mix.append(jnp.dot(p.astype(jnp.bfloat16), own_v[...], preferred_element_type=jnp.float32))
        for b, pieces in enumerate(got):
            p = jnp.exp2(scores[i % 2, b] - top)
            total.append(fold(p, keys, jnp.add))
            values = pieces[:, 1].reshape(each * keys, size)
            mix.append(jnp.dot(p.astype(jnp.bfloat16), values, preferred_element_type=jnp.float32))
        total = jnp.sum(functools.reduce(jnp.add, total), axis=1, keepdims=True)
        normal = functools.reduce(jnp.add, mix) / total
        mine = to_lines(top + jnp.log2(total), eye)
        if not own:
            mine = jnp.where(any_valid > 0, mine, LOW)
        if earlier:
            old, logs = before[0][here, :], before[1][spots, :]
            peak = jnp.maximum(logs, mine)
            power = jnp.exp2(logs - peak)
            whole = power + jnp.exp2(mine - peak)
            normal = normal + to_column(power / whole, eye) * (old - normal)
            mine = peak + jnp.log2(whole)
        if mode == "state":
            outs[0][here, :] = normal
            outs[1][spots, :] = mine
        else:
            outs[i][:rows_step, :] = normal.astype(jnp.bfloat16)
            lse[spots, :] = mine
    if mode == "packed":
        left = lse[...]
        for n in range(3):
            part = left.astype(jnp.bfloat16)
            outs[0][pl.ds(rows_step + n * lines, lines), :] = part
            left = left - part.astype(jnp.float32)


def attend(name, mode, heads, q, valid, got, own=None, earlier=None, cost=COST):
    rows, size = q.shape
    sources = list(got)
    each, _, keys, _ = got[sources[0]].shape
    rows_step = rows // 2
    lines = rows // keys
    scale = size ** -0.5 * math.log2(math.e)
    settings = (own is not None, heads, rows_step, sources, scale, mode, earlier is not None)
    smem = pl.BlockSpec(memory_space=pltpu.SMEM)
    vmem = pl.BlockSpec(memory_space=pltpu.VMEM)
    operands = [q, valid] + list(own or ()) + list(got.values()) + list(earlier or ())
    if mode == "state":
        out_shape = [
            jax.ShapeDtypeStruct((rows, size), jnp.float32),
            jax.ShapeDtypeStruct((lines, keys), jnp.float32),
        ]
    else:
        out_shape = [jax.ShapeDtypeStruct((n, size), jnp.bfloat16) for n in (rows // 2 + 3 * lines, rows // 2)]
    limit = min(VMEM_MOST, VMEM_SMALL + 8 * len(sources) * rows_step * each * keys)
    return pl.pallas_call(
        functools.partial(attend_kernel, settings),
        out_shape=out_shape,
        in_specs=[vmem, smem] + [vmem] * (len(operands) - 2),
        out_specs=[vmem] * len(out_shape),
        scratch_shapes=[
            pltpu.VMEM((2, len(sources), rows_step, each * keys), jnp.float32),
            pltpu.VMEM((2, rows_step if own is not None else 8, own[0].shape[0] if own else keys), jnp.float32),
            pltpu.VMEM((rows_step, size), jnp.float32),
            pltpu.VMEM((lines, keys), jnp.float32),
        ],
        compiler_params=pltpu.CompilerParams(vmem_limit_bytes=limit),
        cost_estimate=cost,
        name=name,
    )(*operands)


def combine_kernel(heads, out_mine, lse_mine, other, more, attended, scratch):
    rows, size = out_mine.shape
    lines, keys = lse_mine.shape
    eye = diagonal(keys)
    mine = lse_mine[...]
    theirs = sum(other[pl.ds(rows // 2 + n * lines, lines), :].astype(jnp.float32) for n in range(3))
    top = jnp.maximum(mine, theirs)
    mine, theirs = jnp.exp2(mine - top), jnp.exp2(theirs - top)
    share = theirs / (mine + theirs)
    for n in range(lines):
        here = pl.ds(n * keys, keys)
        a = out_mine[here, :]
        b = other[here, :] if n < lines // 2 else more[pl.ds((n - lines // 2) * keys, keys), :]
        scratch[here, :] = a + to_column(share[n : n + 1], eye) * (b.astype(jnp.float32) - a)
    tokens = rows // heads
    for h in range(heads):
        attended[:, h * size : (h + 1) * size] = scratch[pl.ds(h, tokens, stride=heads), :].astype(attended.dtype)


def combine(state, parts, heads):
    rows, size = state[0].shape
    vmem = pl.BlockSpec(memory_space=pltpu.VMEM)
    return pl.pallas_call(
        functools.partial(combine_kernel, heads),
        out_shape=jax.ShapeDtypeStruct((rows // heads, heads * size), jnp.bfloat16),
        in_specs=[vmem] * 4,
        out_specs=vmem,
        scratch_shapes=[pltpu.VMEM((rows, size), jnp.float32)],
        compiler_params=pltpu.CompilerParams(vmem_limit_bytes=VMEM_SMALL),
        cost_estimate=LONG,
        name="combine",
    )(*state, *parts)


def project_kernel(attended, w_mine, w_sooner, w_later, away, keep, scratch):
    core = lax.axis_index("head")
    share = away.shape[1]
    cut = w_sooner.shape[0]

    def dot(x, w):
        return jnp.dot(x, w[...], preferred_element_type=jnp.float32)

    scratch[0] = dot(attended[...], w_mine)
    scratch[1] = dot(attended[:, :cut], w_sooner) + dot(attended[:, cut:], w_later)
    for side in range(2):
        away[side] = scratch[side, pl.ds(pl.multiple_of((core ^ 1) * share, share), share), :].astype(jnp.bfloat16)
        keep[side] = scratch[side, pl.ds(pl.multiple_of(core * share, share), share), :]


def project(attended, w_mine, w_sooner, w_later, cores):
    tokens, depth = attended.shape
    width = w_mine.shape[1]
    share = tokens // cores
    vmem = pl.BlockSpec(memory_space=pltpu.VMEM)
    return pl.pallas_call(
        project_kernel,
        out_shape=[
            jax.ShapeDtypeStruct((2, share, width), jnp.bfloat16),
            jax.ShapeDtypeStruct((2, share, width), jnp.float32),
        ],
        in_specs=[vmem] * 4,
        out_specs=[vmem] * 2,
        scratch_shapes=[pltpu.VMEM((2, tokens, width), jnp.float32)],
        compiler_params=pltpu.CompilerParams(vmem_limit_bytes=VMEM_SMALL),
        cost_estimate=COST,
        name="project",
    )(attended, w_mine, w_sooner, w_later)


def place_kernel(masks, *refs):
    parts, out = refs[:-1], refs[-1]
    me = lax.axis_index("req")
    width = parts[0].shape[2]
    for part, mask in zip(parts, masks):
        for side in range(2):
            column = ((me ^ mask) ^ side) * width
            out[:, pl.ds(pl.multiple_of(column, width), width)] = part[side]


def place(parts, masks):
    _, rows, width = parts[0].shape
    vmem = pl.BlockSpec(memory_space=pltpu.VMEM)
    return pl.pallas_call(
        functools.partial(place_kernel, masks),
        out_shape=jax.ShapeDtypeStruct((rows, 2 * len(parts) * width), parts[0].dtype),
        in_specs=[vmem] * len(parts),
        out_specs=vmem,
        compiler_params=pltpu.CompilerParams(vmem_limit_bytes=VMEM_SMALL),
        cost_estimate=COST,
        name="place_columns",
    )(*parts)


def after(value, *others):
    return lax.optimization_barrier((value, others))[0]


def local(queries, new_keys, new_values, cluster_kv, cluster_len, piece_slot, cluster_ids, w_out):
    me = lax.axis_index("req")
    peers = lax.axis_size("req")
    cores = lax.axis_size("head")
    tokens, heads, size = queries.shape
    held = cluster_kv.shape[0]
    keys = cluster_kv.shape[3]
    pieces = piece_slot.shape[1]
    per_peer = pieces // peers
    half = peers // 2
    masks = list(range(1, half))
    last, late, early = masks[-1:], masks[-2:-1], masks[:-2]

    plan = cluster_ids[:, 0]
    first = pack(piece_slot, plan.T, cluster_kv, [m ^ half for m in masks], per_peer)
    got = {m: swap(a, "req", peers, m) for a, m in zip(first, masks)}
    q_mine = queries.reshape(tokens * heads, size)
    q_theirs = swap(q_mine, "req", peers, half)
    second = pack(piece_slot, plan.T, after(cluster_kv, *first), [half, 0] + masks, per_peer)
    got[0], own_pieces, second = second[0], second[1], dict(zip(masks, second[2:]))

    owner = piece_slot // held
    position = jnp.arange(pieces, dtype=jnp.int32)
    same = (owner[:, :, None] == owner[:, None, :]) & (position[:, None] > position[None, :])[None]
    rank = jnp.sum(same.astype(jnp.int32), axis=2)

    def table(request):
        chosen = lax.dynamic_index_in_dim(plan, request, 0, keepdims=False)
        sender = me ^ jnp.arange(half, dtype=jnp.int32)
        fits = (owner[chosen][None, :, None, :] == sender[:, None, None, None]) & (
            rank[chosen][None, :, None, :] == jnp.arange(per_peer, dtype=jnp.int32)[None, None, :, None]
        )
        filled = jnp.clip(cluster_len[chosen][:, None] - position[None, :] * keys, 0, keys)
        return jnp.sum(jnp.where(fits, filled[None, :, None, :], 0), axis=3).reshape(half, -1)

    valid_theirs, valid_mine = table(me ^ half), table(me)

    def some(chosen):
        return {m: got[m] for m in chosen}

    own = attend(
        "attend_own_local", "state", heads, q_mine, valid_mine, {0: own_pieces}, (new_keys[:, 0], new_values[:, 0])
    )
    q_theirs = after(q_theirs, *own)
    state = attend("attend_partner_local", "state", heads, q_theirs, valid_theirs, some([0]), cost=SHORT)
    if early:
        state = attend("attend_partner_early", "state", heads, q_theirs, valid_theirs, some(early), earlier=state)
    got_mine = {m: swap(after(second[m], *state), "req", peers, m) for m in masks}
    state = attend("attend_partner_late", "state", heads, q_theirs, valid_theirs, some(late), earlier=state)
    part = attend("attend_partner_last", "packed", heads, q_theirs, valid_theirs, some(last), earlier=state)
    got = got_mine
    cut = w_out.shape[0] * 3 // 16
    w_sooner = swap(after(w_out[:cut], *part), "req", peers, 1)
    own = after(own, *part)
    part = [swap(a, "req", peers, half) for a in part]

    if early:
        own = attend("attend_own_early", "state", heads, q_mine, valid_mine, some(early), earlier=own)
    own = after(own, w_sooner)
    own = attend("attend_own_late", "state", heads, q_mine, valid_mine, some(late), earlier=own)
    w_later = swap(after(w_out[cut:], *own), "req", peers, 1)
    own = attend("attend_own_last", "state", heads, q_mine, valid_mine, some(last), earlier=own)
    attended = combine(own, part, heads)

    have = {0: attended}
    bit = half
    while bit > 1:
        for mask in list(have):
            rows = after(have[mask], have[bit]) if mask else attended
            have[mask ^ bit] = swap(rows, "req", peers, bit)
        bit //= 2

    single = [m for m in have if m and not m & (m - 1)]
    results, last = {}, ()
    for mask in sorted(have, key=lambda m: (m not in single + [0], m)):
        if mask in single + [0]:
            rows = after(have[mask], *[have[m] for m in single])
        else:
            rows = after(have[mask], *last, *[results[m] for m in single if m != half])
        away, keep = last = project(rows, w_out, w_sooner, w_later, cores)
        away = swap(away, "head", cores, 1)
        summed = (keep + away.astype(jnp.float32)).astype(jnp.bfloat16)
        results[mask] = swap(summed, "req", peers, mask) if mask else summed
    return place(list(results.values()), list(results))


def solution(mesh):
    return jax.shard_map(
        local,
        mesh=mesh,
        in_specs=(
            P(("groups", "req"), "head", None),
            P(("groups", "req"), "head", None),
            P(("groups", "req"), "head", None),
            P(("groups", "req"), "head", None, None, None),
            P("groups"),
            P("groups", None),
            P("groups", "head", None),
            P("head", "req"),
        ),
        out_specs=P(("groups", "req", "head"), None),
        check_vma=False,
    )
```

```python
import functools
import math

import jax
import jax.numpy as jnp
from jax import lax
from jax.experimental import pallas as pl
from jax.experimental.pallas import tpu as pltpu
from jax.sharding import PartitionSpec as P

LOW = -1e30
VMEM_SMALL = 16 * 1024 * 1024
VMEM_MOST = 60 * 1024 * 1024
COST = pl.CostEstimate(flops=1024, bytes_accessed=1024, transcendentals=0)
SHORT = pl.CostEstimate(flops=1 << 31, bytes_accessed=1024, transcendentals=0)
LONG = pl.CostEstimate(flops=1 << 40, bytes_accessed=1024, transcendentals=0)


def swap(array, axis, size, mask):
    return lax.ppermute(array, axis, [(i, i ^ mask) for i in range(size)])


def pack_kernel(wanted, per_peer, slot_ref, ids_ref, kv_ref, *rest):
    outs, (slots, ids, table, sems, first) = rest[:-5], rest[-5:]
    loads = [
        pltpu.make_async_copy(slot_ref, slots, first.at[0]),
        pltpu.make_async_copy(ids_ref, ids, first.at[1]),
    ]
    for copy in loads:
        copy.start()
    for copy in loads:
        copy.wait()
    me = lax.axis_index("req")
    pieces = slots.shape[1]
    held = kv_ref.shape[0]
    picks = ids.shape[0]
    low = me * held
    copies = []
    for out, mask in zip(outs, wanted):
        for s in range(picks):
            row = (len(copies) // per_peer) % table.shape[0]
            c = ids[s, me ^ mask]

            def scan(p, count, c=c, row=row):
                slot = slots[c, p] - low
                table[row, count] = slot
                return count + ((slot >= 0) & (slot < held)).astype(jnp.int32)

            lax.fori_loop(0, pieces, scan, jnp.int32(0), unroll=8)
            for k in range(per_peer):
                copies.append(
                    pltpu.make_async_copy(kv_ref.at[table[row, k], 0], out.at[s * per_peer + k], sems.at[len(copies)])
                )
                copies[-1].start()
    for copy in copies:
        copy.wait()


def pack(piece_slot, plan, cluster_kv, wanted, per_peer):
    count = plan.shape[0] * per_peer
    shape = jax.ShapeDtypeStruct((count,) + cluster_kv.shape[2:], cluster_kv.dtype)
    hbm = pl.BlockSpec(memory_space=pltpu.HBM)
    total = len(wanted)
    return pl.pallas_call(
        functools.partial(pack_kernel, wanted, per_peer),
        out_shape=[shape] * total,
        in_specs=[hbm] * 3,
        out_specs=[pl.BlockSpec(memory_space=pltpu.VMEM)] * total,
        scratch_shapes=[
            pltpu.SMEM(piece_slot.shape, jnp.int32),
            pltpu.SMEM(plan.shape, jnp.int32),
            pltpu.SMEM((total * plan.shape[0], per_peer + 1), jnp.int32),
            pltpu.SemaphoreType.DMA((total * count,)),
            pltpu.SemaphoreType.DMA((2,)),
        ],
        compiler_params=pltpu.CompilerParams(vmem_limit_bytes=VMEM_MOST),
        cost_estimate=COST,
        name="pack_pieces",
    )(piece_slot, plan, cluster_kv)


def fold(values, keys, op):
    parts = [values[:, i * keys : (i + 1) * keys] for i in range(values.shape[1] // keys)]
    while len(parts) > 1:
        parts = [op(parts[i], parts[i + 1]) if i + 1 < len(parts) else parts[i] for i in range(0, len(parts), 2)]
    return parts[0]


def to_lines(column, eye):
    keys = eye.shape[0]
    return jnp.concatenate(
        [
            jnp.sum(jnp.where(eye, column[n : n + keys], 0.0), axis=0, keepdims=True)
            for n in range(0, column.shape[0], keys)
        ],
        axis=0,
    )


def to_column(lines, eye):
    return jnp.concatenate(
        [jnp.sum(jnp.where(eye, lines[n : n + 1], 0.0), axis=1, keepdims=True) for n in range(lines.shape[0])],
        axis=0,
    )


def diagonal(keys):
    return lax.broadcasted_iota(jnp.int32, (keys, keys), 0) == lax.broadcasted_iota(jnp.int32, (keys, keys), 1)


def attend_kernel(settings, *refs):
    own, heads, rows_step, sources, scale, mode, earlier = settings
    refs = list(refs)

    def take(n):
        taken, refs[:] = refs[:n], refs[n:]
        return taken

    q_ref, valid_ref = take(2)
    own_k, own_v = take(2) if own else (None, None)
    got = take(len(sources))
    before = take(2) if earlier else None
    outs = take(2)
    scores, own_scores, tops, lse = refs
    rows, size = q_ref.shape
    each, _, keys, _ = got[0].shape
    lines = rows // keys
    group = rows_step // keys
    steps = rows // rows_step
    lane = lax.broadcasted_iota(jnp.int32, (1, keys), 1)
    eye = diagonal(keys)
    biases, any_valid = [], jnp.int32(0)
    for j in sources:
        valid = [valid_ref[j, e] for e in range(each)]
        biases.append(jnp.concatenate([jnp.where(lane < v, 0.0, LOW) for v in valid], axis=1))
        any_valid = sum(valid, any_valid)

    def dot_t(x, y):
        return lax.dot_general(x, y, (((1,), (1,)), ((), ())), preferred_element_type=jnp.float32)

    def score(i, turn):
        q = q_ref[pl.ds(pl.multiple_of(i * rows_step, rows_step), rows_step), :]
        found = []
        if own:
            s = dot_t(q, own_k[...])
            position = (lax.broadcasted_iota(jnp.int32, s.shape, 0) + i * rows_step) // heads
            s = jnp.where(position >= lax.broadcasted_iota(jnp.int32, s.shape, 1), s * scale, LOW)
            own_scores[turn] = s
            found.append(s)
        for b, pieces in enumerate(got):
            s = dot_t(q, pieces[:, 0].reshape(each * keys, size)) * scale + biases[b]
            scores[turn, b] = s
            found.append(fold(s, keys, jnp.maximum))
        tops[turn] = functools.reduce(jnp.maximum, found)

    def weigh(i, turn):
        here = pl.ds(pl.multiple_of(i * rows_step, rows_step), rows_step)
        top = jnp.max(tops[turn], axis=1, keepdims=True)
        total, mix = [], []
        if own:
            p = jnp.exp2(own_scores[turn] - top)
            total.append(fold(p, keys, jnp.add))
            mix.append(jnp.dot(p.astype(jnp.bfloat16), own_v[...], preferred_element_type=jnp.float32))
        for b, pieces in enumerate(got):
            p = jnp.exp2(scores[turn, b] - top)
            total.append(fold(p, keys, jnp.add))
            values = pieces[:, 1].reshape(each * keys, size)
            mix.append(jnp.dot(p.astype(jnp.bfloat16), values, preferred_element_type=jnp.float32))
        total = jnp.sum(functools.reduce(jnp.add, total), axis=1, keepdims=True)
        normal = functools.reduce(jnp.add, mix) / total
        mine = to_lines(top + jnp.log2(total), eye)
        if not own:
            mine = jnp.where(any_valid > 0, mine, LOW)
        if earlier:
            old, logs = before[0][here, :], before[1][i]
            peak = jnp.maximum(logs, mine)
            power = jnp.exp2(logs - peak)
            whole = power + jnp.exp2(mine - peak)
            normal = normal + to_column(power / whole, eye) * (old - normal)
            mine = peak + jnp.log2(whole)
        if mode == "state":
            outs[0][here, :] = normal
            outs[1][i] = mine
        else:
            lse[i] = mine
            low = normal.astype(jnp.bfloat16)
            for n in range(2):

                @pl.when(i // (steps // 2) == n)
                def _(n=n):
                    spot = pl.multiple_of((i - n * (steps // 2)) * rows_step, rows_step)
                    outs[n][pl.ds(spot, rows_step), :] = low

    score(0, 0)

    def each_step(i, carry):
        for turn in range(2):
            score(jnp.minimum(2 * i + turn + 1, steps - 1), 1 - turn)
            weigh(2 * i + turn, turn)
        return carry

    lax.fori_loop(0, steps // 2, each_step, 0)
    if mode == "packed":
        left = jnp.concatenate([lse[i] for i in range(steps)], axis=0)
        for n in range(3):
            part = left.astype(jnp.bfloat16)
            outs[0][pl.ds(rows // 2 + n * lines, lines), :] = part
            left = left - part.astype(jnp.float32)


def attend(name, mode, heads, q, valid, got, own=None, earlier=None, cost=COST):
    rows, size = q.shape
    sources = list(got)
    each, _, keys, _ = got[sources[0]].shape
    rows_step = math.gcd(rows, 512)
    lines = rows // keys
    scale = size ** -0.5 * math.log2(math.e)
    settings = (own is not None, heads, rows_step, sources, scale, mode, earlier is not None)
    smem = pl.BlockSpec(memory_space=pltpu.SMEM)
    vmem = pl.BlockSpec(memory_space=pltpu.VMEM)
    operands = [q, valid] + list(own or ()) + list(got.values()) + list(earlier or ())
    if mode == "state":
        out_shape = [
            jax.ShapeDtypeStruct((rows, size), jnp.float32),
            jax.ShapeDtypeStruct((rows // rows_step, rows_step // keys, keys), jnp.float32),
        ]
    else:
        out_shape = [jax.ShapeDtypeStruct((n, size), jnp.bfloat16) for n in (rows // 2 + 3 * lines, rows // 2)]
    limit = min(VMEM_MOST, VMEM_SMALL + 8 * len(sources) * rows_step * each * keys)
    return pl.pallas_call(
        functools.partial(attend_kernel, settings),
        out_shape=out_shape,
        in_specs=[vmem, smem] + [vmem] * (len(operands) - 2),
        out_specs=[vmem] * len(out_shape),
        scratch_shapes=[
            pltpu.VMEM((2, len(sources), rows_step, each * keys), jnp.float32),
            pltpu.VMEM((2, rows_step if own is not None else 8, own[0].shape[0] if own else keys), jnp.float32),
            pltpu.VMEM((2, rows_step, keys), jnp.float32),
            pltpu.VMEM((rows // rows_step, rows_step // keys, keys), jnp.float32),
        ],
        compiler_params=pltpu.CompilerParams(vmem_limit_bytes=limit),
        cost_estimate=cost,
        name=name,
    )(*operands)


def combine_kernel(heads, out_mine, lse_mine, other, more, attended, scratch):
    rows, size = out_mine.shape
    steps, group, keys = lse_mine.shape
    lines = steps * group
    eye = diagonal(keys)
    mine = jnp.concatenate([lse_mine[i] for i in range(steps)], axis=0)
    theirs = sum(other[pl.ds(rows // 2 + n * lines, lines), :].astype(jnp.float32) for n in range(3))
    top = jnp.maximum(mine, theirs)
    mine, theirs = jnp.exp2(mine - top), jnp.exp2(theirs - top)
    share = theirs / (mine + theirs)
    for n in range(lines):
        here = pl.ds(n * keys, keys)
        a = out_mine[here, :]
        b = other[here, :] if n < lines // 2 else more[pl.ds((n - lines // 2) * keys, keys), :]
        scratch[here, :] = a + to_column(share[n : n + 1], eye) * (b.astype(jnp.float32) - a)
    tokens = rows // heads
    for h in range(heads):
        attended[:, h * size : (h + 1) * size] = scratch[pl.ds(h, tokens, stride=heads), :].astype(attended.dtype)


def combine(state, parts, heads):
    rows, size = state[0].shape
    vmem = pl.BlockSpec(memory_space=pltpu.VMEM)
    return pl.pallas_call(
        functools.partial(combine_kernel, heads),
        out_shape=jax.ShapeDtypeStruct((rows // heads, heads * size), jnp.bfloat16),
        in_specs=[vmem] * 4,
        out_specs=vmem,
        scratch_shapes=[pltpu.VMEM((rows, size), jnp.float32)],
        compiler_params=pltpu.CompilerParams(vmem_limit_bytes=VMEM_SMALL),
        cost_estimate=LONG,
        name="combine",
    )(*state, *parts)


def project_kernel(attended, w_mine, w_sooner, w_later, away, keep, scratch):
    core = lax.axis_index("head")
    share = away.shape[1]
    cut = w_sooner.shape[0]

    def dot(x, w):
        return jnp.dot(x, w[...], preferred_element_type=jnp.float32)

    scratch[0] = dot(attended[...], w_mine)
    scratch[1] = dot(attended[:, :cut], w_sooner) + dot(attended[:, cut:], w_later)
    for side in range(2):
        away[side] = scratch[side, pl.ds(pl.multiple_of((core ^ 1) * share, share), share), :].astype(jnp.bfloat16)
        keep[side] = scratch[side, pl.ds(pl.multiple_of(core * share, share), share), :]


def project(attended, w_mine, w_sooner, w_later, cores):
    tokens, depth = attended.shape
    width = w_mine.shape[1]
    share = tokens // cores
    vmem = pl.BlockSpec(memory_space=pltpu.VMEM)
    return pl.pallas_call(
        project_kernel,
        out_shape=[
            jax.ShapeDtypeStruct((2, share, width), jnp.bfloat16),
            jax.ShapeDtypeStruct((2, share, width), jnp.float32),
        ],
        in_specs=[vmem] * 4,
        out_specs=[vmem] * 2,
        scratch_shapes=[pltpu.VMEM((2, tokens, width), jnp.float32)],
        compiler_params=pltpu.CompilerParams(vmem_limit_bytes=VMEM_SMALL),
        cost_estimate=COST,
        name="project",
    )(attended, w_mine, w_sooner, w_later)


def place_kernel(masks, *refs):
    parts, out = refs[:-1], refs[-1]
    me = lax.axis_index("req")
    width = parts[0].shape[2]
    for part, mask in zip(parts, masks):
        for side in range(2):
            column = ((me ^ mask) ^ side) * width
            out[:, pl.ds(pl.multiple_of(column, width), width)] = part[side]


def place(parts, masks):
    _, rows, width = parts[0].shape
    vmem = pl.BlockSpec(memory_space=pltpu.VMEM)
    return pl.pallas_call(
        functools.partial(place_kernel, masks),
        out_shape=jax.ShapeDtypeStruct((rows, 2 * len(parts) * width), parts[0].dtype),
        in_specs=[vmem] * len(parts),
        out_specs=vmem,
        compiler_params=pltpu.CompilerParams(vmem_limit_bytes=VMEM_SMALL),
        cost_estimate=COST,
        name="place_columns",
    )(*parts)


def after(value, *others):
    return lax.optimization_barrier((value, others))[0]


def local(queries, new_keys, new_values, cluster_kv, cluster_len, piece_slot, cluster_ids, w_out):
    me = lax.axis_index("req")
    peers = lax.axis_size("req")
    cores = lax.axis_size("head")
    tokens, heads, size = queries.shape
    held = cluster_kv.shape[0]
    keys = cluster_kv.shape[3]
    pieces = piece_slot.shape[1]
    per_peer = pieces // peers
    half = peers // 2
    masks = list(range(1, half))
    last, late, early = masks[-1:], masks[-2:-1], masks[:-2]

    plan = cluster_ids[:, 0]
    first = pack(piece_slot, plan.T, cluster_kv, [m ^ half for m in masks], per_peer)
    got = {m: swap(a, "req", peers, m) for a, m in zip(first, masks)}
    q_mine = queries.reshape(tokens * heads, size)
    q_theirs = swap(q_mine, "req", peers, half)
    second = pack(piece_slot, plan.T, after(cluster_kv, *first), [half, 0] + masks, per_peer)
    got[0], own_pieces, second = second[0], second[1], dict(zip(masks, second[2:]))

    owner = piece_slot // held
    position = jnp.arange(pieces, dtype=jnp.int32)
    same = (owner[:, :, None] == owner[:, None, :]) & (position[:, None] > position[None, :])[None]
    rank = jnp.sum(same.astype(jnp.int32), axis=2)

    def table(request):
        chosen = lax.dynamic_index_in_dim(plan, request, 0, keepdims=False)
        sender = me ^ jnp.arange(half, dtype=jnp.int32)
        fits = (owner[chosen][None, :, None, :] == sender[:, None, None, None]) & (
            rank[chosen][None, :, None, :] == jnp.arange(per_peer, dtype=jnp.int32)[None, None, :, None]
        )
        filled = jnp.clip(cluster_len[chosen][:, None] - position[None, :] * keys, 0, keys)
        return jnp.sum(jnp.where(fits, filled[None, :, None, :], 0), axis=3).reshape(half, -1)

    valid_theirs, valid_mine = table(me ^ half), table(me)

    def some(chosen):
        return {m: got[m] for m in chosen}

    own = attend(
        "attend_own_local", "state", heads, q_mine, valid_mine, {0: own_pieces}, (new_keys[:, 0], new_values[:, 0])
    )
    q_theirs = after(q_theirs, *own)
    state = attend("attend_partner_local", "state", heads, q_theirs, valid_theirs, some([0]), cost=SHORT)
    if early:
        state = attend("attend_partner_early", "state", heads, q_theirs, valid_theirs, some(early), earlier=state)
    got_mine = {m: swap(after(second[m], *state), "req", peers, m) for m in masks}
    state = attend("attend_partner_late", "state", heads, q_theirs, valid_theirs, some(late), earlier=state)
    part = attend("attend_partner_last", "packed", heads, q_theirs, valid_theirs, some(last), earlier=state)
    got = got_mine
    cut = w_out.shape[0] * 3 // 16
    w_sooner = swap(after(w_out[:cut], *part), "req", peers, 1)
    own = after(own, *part)
    part = [swap(a, "req", peers, half) for a in part]

    if early:
        own = attend("attend_own_early", "state", heads, q_mine, valid_mine, some(early), earlier=own)
    own = after(own, w_sooner)
    own = attend("attend_own_late", "state", heads, q_mine, valid_mine, some(late), earlier=own)
    w_later = swap(after(w_out[cut:], *own), "req", peers, 1)
    own = attend("attend_own_last", "state", heads, q_mine, valid_mine, some(last), earlier=own)
    attended = combine(own, part, heads)

    have = {0: attended}
    bit = half
    while bit > 1:
        for mask in list(have):
            rows = after(have[mask], have[bit]) if mask else attended
            have[mask ^ bit] = swap(rows, "req", peers, bit)
        bit //= 2

    single = [m for m in have if m and not m & (m - 1)]
    results, last = {}, ()
    for mask in sorted(have, key=lambda m: (m not in single + [0], -m)):
        if mask in single + [0]:
            rows = after(have[mask], *[have[m] for m in single])
        else:
            rows = after(have[mask], *last, *[results[m] for m in single if m != half])
        away, keep = last = project(rows, w_out, w_sooner, w_later, cores)
        away = swap(away, "head", cores, 1)
        summed = (keep + away.astype(jnp.float32)).astype(jnp.bfloat16)
        results[mask] = swap(summed, "req", peers, mask) if mask else summed
    return place(list(results.values()), list(results))


def solution(mesh):
    return jax.shard_map(
        local,
        mesh=mesh,
        in_specs=(
            P(("groups", "req"), "head", None),
            P(("groups", "req"), "head", None),
            P(("groups", "req"), "head", None),
            P(("groups", "req"), "head", None, None, None),
            P("groups"),
            P("groups", None),
            P("groups", "head", None),
            P("head", "req"),
        ),
        out_specs=P(("groups", "req", "head"), None),
        check_vma=False,
    )
```

```python
import functools
import math

import jax
import jax.numpy as jnp
from jax import lax
from jax.experimental import pallas as pl
from jax.experimental.pallas import tpu as pltpu
from jax.sharding import PartitionSpec as P

LOW = -1e30
VMEM_SMALL = 16 * 1024 * 1024
VMEM_MOST = 60 * 1024 * 1024
COST = pl.CostEstimate(flops=1024, bytes_accessed=1024, transcendentals=0)
SHORT = pl.CostEstimate(flops=1 << 31, bytes_accessed=1024, transcendentals=0)
LONG = pl.CostEstimate(flops=1 << 40, bytes_accessed=1024, transcendentals=0)


def swap(array, axis, size, mask):
    return lax.ppermute(array, axis, [(i, i ^ mask) for i in range(size)])


def pack_kernel(wanted, per_peer, slot_ref, ids_ref, kv_ref, *rest):
    outs, (slots, ids, table, sems, first) = rest[:-5], rest[-5:]
    loads = [
        pltpu.make_async_copy(slot_ref, slots, first.at[0]),
        pltpu.make_async_copy(ids_ref, ids, first.at[1]),
    ]
    for copy in loads:
        copy.start()
    for copy in loads:
        copy.wait()
    me = lax.axis_index("req")
    pieces = slots.shape[1]
    held = kv_ref.shape[0]
    picks = ids.shape[0]
    low = me * held
    copies = []
    for out, mask in zip(outs, wanted):
        for s in range(picks):
            row = (len(copies) // per_peer) % table.shape[0]
            c = ids[s, me ^ mask]

            def scan(p, count, c=c, row=row):
                slot = slots[c, p] - low
                table[row, count] = slot
                return count + ((slot >= 0) & (slot < held)).astype(jnp.int32)

            lax.fori_loop(0, pieces, scan, jnp.int32(0), unroll=8)
            for k in range(per_peer):
                copies.append(
                    pltpu.make_async_copy(kv_ref.at[table[row, k], 0], out.at[s * per_peer + k], sems.at[len(copies)])
                )
                copies[-1].start()
    for copy in copies:
        copy.wait()


def pack(piece_slot, plan, cluster_kv, wanted, per_peer):
    count = plan.shape[0] * per_peer
    shape = jax.ShapeDtypeStruct((count,) + cluster_kv.shape[2:], cluster_kv.dtype)
    hbm = pl.BlockSpec(memory_space=pltpu.HBM)
    total = len(wanted)
    return pl.pallas_call(
        functools.partial(pack_kernel, wanted, per_peer),
        out_shape=[shape] * total,
        in_specs=[hbm] * 3,
        out_specs=[pl.BlockSpec(memory_space=pltpu.VMEM)] * total,
        scratch_shapes=[
            pltpu.SMEM(piece_slot.shape, jnp.int32),
            pltpu.SMEM(plan.shape, jnp.int32),
            pltpu.SMEM((total * plan.shape[0], per_peer + 1), jnp.int32),
            pltpu.SemaphoreType.DMA((total * count,)),
            pltpu.SemaphoreType.DMA((2,)),
        ],
        compiler_params=pltpu.CompilerParams(vmem_limit_bytes=VMEM_MOST),
        cost_estimate=COST,
        name="pack_pieces",
    )(piece_slot, plan, cluster_kv)


def fold(values, keys, op):
    parts = [values[:, i * keys : (i + 1) * keys] for i in range(values.shape[1] // keys)]
    while len(parts) > 1:
        parts = [op(parts[i], parts[i + 1]) if i + 1 < len(parts) else parts[i] for i in range(0, len(parts), 2)]
    return parts[0]


def to_lines(column, eye):
    keys = eye.shape[0]
    return jnp.concatenate(
        [
            jnp.sum(jnp.where(eye, column[n : n + keys], 0.0), axis=0, keepdims=True)
            for n in range(0, column.shape[0], keys)
        ],
        axis=0,
    )


def to_column(lines, eye):
    return jnp.concatenate(
        [jnp.sum(jnp.where(eye, lines[n : n + 1], 0.0), axis=1, keepdims=True) for n in range(lines.shape[0])],
        axis=0,
    )


def diagonal(keys):
    return lax.broadcasted_iota(jnp.int32, (keys, keys), 0) == lax.broadcasted_iota(jnp.int32, (keys, keys), 1)


def attend_kernel(settings, *refs):
    own, heads, rows_step, sources, scale, mode, earlier = settings
    refs = list(refs)

    def take(n):
        taken, refs[:] = refs[:n], refs[n:]
        return taken

    q_ref, valid_ref = take(2)
    own_k, own_v = take(2) if own else (None, None)
    got = take(len(sources))
    before = take(2) if earlier else None
    outs = take(2)
    scores, own_scores, tops, lse = refs
    rows, size = q_ref.shape
    each, _, keys, _ = got[0].shape
    lines = rows // keys
    group = rows_step // keys
    steps = rows // rows_step
    lane = lax.broadcasted_iota(jnp.int32, (1, keys), 1)
    eye = diagonal(keys)
    biases, any_valid = [], jnp.int32(0)
    for j in sources:
        valid = [valid_ref[j, e] for e in range(each)]
        biases.append(jnp.concatenate([jnp.where(lane < v, 0.0, LOW) for v in valid], axis=1))
        any_valid = sum(valid, any_valid)

    def dot_t(x, y):
        return lax.dot_general(x, y, (((1,), (1,)), ((), ())), preferred_element_type=jnp.float32)

    def score(i, turn):
        q = q_ref[pl.ds(pl.multiple_of(i * rows_step, rows_step), rows_step), :]
        found = []
        if own:
            s = dot_t(q, own_k[...])
            position = (lax.broadcasted_iota(jnp.int32, s.shape, 0) + i * rows_step) // heads
            s = jnp.where(position >= lax.broadcasted_iota(jnp.int32, s.shape, 1), s * scale, LOW)
            own_scores[turn] = s
            found.append(s)
        for b, pieces in enumerate(got):
            s = dot_t(q, pieces[:, 0].reshape(each * keys, size)) * scale + biases[b]
            scores[turn, b] = s
            found.append(fold(s, keys, jnp.maximum))
        tops[turn] = functools.reduce(jnp.maximum, found)

    def weigh(i, turn):
        here = pl.ds(pl.multiple_of(i * rows_step, rows_step), rows_step)
        top = jnp.max(tops[turn], axis=1, keepdims=True)
        total, mix = [], []
        if own:
            p = jnp.exp2(own_scores[turn] - top)
            total.append(fold(p, keys, jnp.add))
            mix.append(jnp.dot(p.astype(jnp.bfloat16), own_v[...], preferred_element_type=jnp.float32))
        for b, pieces in enumerate(got):
            p = jnp.exp2(scores[turn, b] - top)
            total.append(fold(p, keys, jnp.add))
            values = pieces[:, 1].reshape(each * keys, size)
            mix.append(jnp.dot(p.astype(jnp.bfloat16), values, preferred_element_type=jnp.float32))
        total = jnp.sum(functools.reduce(jnp.add, total), axis=1, keepdims=True)
        normal = functools.reduce(jnp.add, mix) / total
        mine = to_lines(top + jnp.log2(total), eye)
        if not own:
            mine = jnp.where(any_valid > 0, mine, LOW)
        if earlier:
            old, logs = before[0][here, :], before[1][i]
            peak = jnp.maximum(logs, mine)
            power = jnp.exp2(logs - peak)
            whole = power + jnp.exp2(mine - peak)
            normal = normal + to_column(power / whole, eye) * (old - normal)
            mine = peak + jnp.log2(whole)
        if mode == "state":
            outs[0][here, :] = normal
            outs[1][i] = mine
        else:
            lse[i] = mine
            low = normal.astype(jnp.bfloat16)
            for n in range(2):

                @pl.when(i // (steps // 2) == n)
                def _(n=n):
                    spot = pl.multiple_of((i - n * (steps // 2)) * rows_step, rows_step)
                    outs[n][pl.ds(spot, rows_step), :] = low

    score(0, 0)

    def each_step(i, carry):
        for turn in range(2):
            score(jnp.minimum(2 * i + turn + 1, steps - 1), 1 - turn)
            weigh(2 * i + turn, turn)
        return carry

    lax.fori_loop(0, steps // 2, each_step, 0)
    if mode == "packed":
        left = jnp.concatenate([lse[i] for i in range(steps)], axis=0)
        for n in range(3):
            part = left.astype(jnp.bfloat16)
            outs[0][pl.ds(rows // 2 + n * lines, lines), :] = part
            left = left - part.astype(jnp.float32)


def attend(name, mode, heads, q, valid, got, own=None, earlier=None, cost=COST):
    rows, size = q.shape
    sources = list(got)
    each, _, keys, _ = got[sources[0]].shape
    rows_step = math.gcd(rows, 512)
    lines = rows // keys
    scale = size ** -0.5 * math.log2(math.e)
    settings = (own is not None, heads, rows_step, sources, scale, mode, earlier is not None)
    smem = pl.BlockSpec(memory_space=pltpu.SMEM)
    vmem = pl.BlockSpec(memory_space=pltpu.VMEM)
    operands = [q, valid] + list(own or ()) + list(got.values()) + list(earlier or ())
    if mode == "state":
        out_shape = [
            jax.ShapeDtypeStruct((rows, size), jnp.float32),
            jax.ShapeDtypeStruct((rows // rows_step, rows_step // keys, keys), jnp.float32),
        ]
    else:
        out_shape = [jax.ShapeDtypeStruct((n, size), jnp.bfloat16) for n in (rows // 2 + 3 * lines, rows // 2)]
    limit = min(VMEM_MOST, VMEM_SMALL + 8 * len(sources) * rows_step * each * keys)
    return pl.pallas_call(
        functools.partial(attend_kernel, settings),
        out_shape=out_shape,
        in_specs=[vmem, smem] + [vmem] * (len(operands) - 2),
        out_specs=[vmem] * len(out_shape),
        scratch_shapes=[
            pltpu.VMEM((2, len(sources), rows_step, each * keys), jnp.float32),
            pltpu.VMEM((2, rows_step if own is not None else 8, own[0].shape[0] if own else keys), jnp.float32),
            pltpu.VMEM((2, rows_step, keys), jnp.float32),
            pltpu.VMEM((rows // rows_step, rows_step // keys, keys), jnp.float32),
        ],
        compiler_params=pltpu.CompilerParams(vmem_limit_bytes=limit),
        cost_estimate=cost,
        name=name,
    )(*operands)


def combine_kernel(heads, out_mine, lse_mine, other, more, attended, scratch):
    rows, size = out_mine.shape
    steps, group, keys = lse_mine.shape
    lines = steps * group
    eye = diagonal(keys)
    mine = jnp.concatenate([lse_mine[i] for i in range(steps)], axis=0)
    theirs = sum(other[pl.ds(rows // 2 + n * lines, lines), :].astype(jnp.float32) for n in range(3))
    top = jnp.maximum(mine, theirs)
    mine, theirs = jnp.exp2(mine - top), jnp.exp2(theirs - top)
    share = theirs / (mine + theirs)
    for n in range(lines):
        here = pl.ds(n * keys, keys)
        a = out_mine[here, :]
        b = other[here, :] if n < lines // 2 else more[pl.ds((n - lines // 2) * keys, keys), :]
        scratch[here, :] = a + to_column(share[n : n + 1], eye) * (b.astype(jnp.float32) - a)
    tokens = rows // heads
    for h in range(heads):
        attended[:, h * size : (h + 1) * size] = scratch[pl.ds(h, tokens, stride=heads), :].astype(attended.dtype)


def combine(state, parts, heads):
    rows, size = state[0].shape
    vmem = pl.BlockSpec(memory_space=pltpu.VMEM)
    return pl.pallas_call(
        functools.partial(combine_kernel, heads),
        out_shape=jax.ShapeDtypeStruct((rows // heads, heads * size), jnp.bfloat16),
        in_specs=[vmem] * 4,
        out_specs=vmem,
        scratch_shapes=[pltpu.VMEM((rows, size), jnp.float32)],
        compiler_params=pltpu.CompilerParams(vmem_limit_bytes=VMEM_SMALL),
        cost_estimate=LONG,
        name="combine",
    )(*state, *parts)


def stage_kernel(source, target, sems):
    rows = source.shape[0] // sems.shape[0]
    copies = []
    for n in range(sems.shape[0]):
        part = pl.ds(n * rows, rows)
        copies.append(pltpu.make_async_copy(source.at[part], target.at[part], sems.at[n]))
        copies[-1].start()
    for copy in copies:
        copy.wait()


def stage(array):
    return pl.pallas_call(
        stage_kernel,
        out_shape=jax.ShapeDtypeStruct(array.shape, array.dtype),
        in_specs=[pl.BlockSpec(memory_space=pl.ANY)],
        out_specs=pl.BlockSpec(memory_space=pltpu.VMEM),
        scratch_shapes=[pltpu.SemaphoreType.DMA((8,))],
        compiler_params=pltpu.CompilerParams(vmem_limit_bytes=VMEM_SMALL),
        cost_estimate=COST,
        name="stage",
    )(array)


def project_kernel(attended, w_mine, w_sooner, w_later, away, keep, scratch):
    core = lax.axis_index("head")
    share = away.shape[1]
    cut = w_sooner.shape[0]

    def dot(x, w):
        return jnp.dot(x, w[...], preferred_element_type=jnp.float32)

    scratch[0] = dot(attended[...], w_mine)
    scratch[1] = dot(attended[:, :cut], w_sooner) + dot(attended[:, cut:], w_later)
    for side in range(2):
        away[side] = scratch[side, pl.ds(pl.multiple_of((core ^ 1) * share, share), share), :].astype(jnp.bfloat16)
        keep[side] = scratch[side, pl.ds(pl.multiple_of(core * share, share), share), :]


def project(attended, w_mine, w_sooner, w_later, cores):
    tokens, depth = attended.shape
    width = w_mine.shape[1]
    share = tokens // cores
    vmem = pl.BlockSpec(memory_space=pltpu.VMEM)
    return pl.pallas_call(
        project_kernel,
        out_shape=[
            jax.ShapeDtypeStruct((2, share, width), jnp.bfloat16),
            jax.ShapeDtypeStruct((2, share, width), jnp.float32),
        ],
        in_specs=[vmem] * 4,
        out_specs=[vmem] * 2,
        scratch_shapes=[pltpu.VMEM((2, tokens, width), jnp.float32)],
        compiler_params=pltpu.CompilerParams(vmem_limit_bytes=VMEM_SMALL),
        cost_estimate=COST,
        name="project",
    )(attended, w_mine, w_sooner, w_later)


def place_kernel(masks, *refs):
    parts, out = refs[:-1], refs[-1]
    me = lax.axis_index("req")
    width = parts[0].shape[2]
    for part, mask in zip(parts, masks):
        for side in range(2):
            column = ((me ^ mask) ^ side) * width
            out[:, pl.ds(pl.multiple_of(column, width), width)] = part[side]


def place(parts, masks):
    _, rows, width = parts[0].shape
    vmem = pl.BlockSpec(memory_space=pltpu.VMEM)
    return pl.pallas_call(
        functools.partial(place_kernel, masks),
        out_shape=jax.ShapeDtypeStruct((rows, 2 * len(parts) * width), parts[0].dtype),
        in_specs=[vmem] * len(parts),
        out_specs=vmem,
        compiler_params=pltpu.CompilerParams(vmem_limit_bytes=VMEM_SMALL),
        cost_estimate=COST,
        name="place_columns",
    )(*parts)


def after(value, *others):
    return lax.optimization_barrier((value, others))[0]


def local(queries, new_keys, new_values, cluster_kv, cluster_len, piece_slot, cluster_ids, w_out):
    me = lax.axis_index("req")
    peers = lax.axis_size("req")
    cores = lax.axis_size("head")
    tokens, heads, size = queries.shape
    held = cluster_kv.shape[0]
    keys = cluster_kv.shape[3]
    pieces = piece_slot.shape[1]
    per_peer = pieces // peers
    half = peers // 2
    masks = list(range(1, half))
    last, late, early = masks[-1:], masks[-2:-1], masks[:-2]

    plan = cluster_ids[:, 0]
    first = pack(piece_slot, plan.T, cluster_kv, [m ^ half for m in masks], per_peer)
    got = {m: swap(a, "req", peers, m) for a, m in zip(first, masks)}
    q_mine = queries.reshape(tokens * heads, size)
    q_theirs = swap(q_mine, "req", peers, half)
    second = pack(piece_slot, plan.T, after(cluster_kv, *first), [half, 0] + masks, per_peer)
    got[0], own_pieces, second = second[0], second[1], dict(zip(masks, second[2:]))

    owner = piece_slot // held
    position = jnp.arange(pieces, dtype=jnp.int32)
    same = (owner[:, :, None] == owner[:, None, :]) & (position[:, None] > position[None, :])[None]
    rank = jnp.sum(same.astype(jnp.int32), axis=2)

    def table(request):
        chosen = lax.dynamic_index_in_dim(plan, request, 0, keepdims=False)
        sender = me ^ jnp.arange(half, dtype=jnp.int32)
        fits = (owner[chosen][None, :, None, :] == sender[:, None, None, None]) & (
            rank[chosen][None, :, None, :] == jnp.arange(per_peer, dtype=jnp.int32)[None, None, :, None]
        )
        filled = jnp.clip(cluster_len[chosen][:, None] - position[None, :] * keys, 0, keys)
        return jnp.sum(jnp.where(fits, filled[None, :, None, :], 0), axis=3).reshape(half, -1)

    valid_theirs, valid_mine = table(me ^ half), table(me)

    def some(chosen):
        return {m: got[m] for m in chosen}

    own = attend(
        "attend_own_local", "state", heads, q_mine, valid_mine, {0: own_pieces}, (new_keys[:, 0], new_values[:, 0])
    )
    q_theirs = after(q_theirs, *own)
    state = attend("attend_partner_local", "state", heads, q_theirs, valid_theirs, some([0]), cost=SHORT)
    if early:
        state = attend("attend_partner_early", "state", heads, q_theirs, valid_theirs, some(early), earlier=state)
    got_mine = {m: swap(after(second[m], *state), "req", peers, m) for m in masks}
    state = attend("attend_partner_late", "state", heads, q_theirs, valid_theirs, some(late), earlier=state)
    part = attend("attend_partner_last", "packed", heads, q_theirs, valid_theirs, some(last), earlier=state)
    got = got_mine
    cut = w_out.shape[0] * 3 // 16
    w_sooner = swap(after(w_out[:cut], *part), "req", peers, 1)
    own = after(own, *part)
    part = [swap(a, "req", peers, half) for a in part]

    if early:
        own = attend("attend_own_early", "state", heads, q_mine, valid_mine, some(early), earlier=own)
    own = after(own, w_sooner)
    own = attend("attend_own_late", "state", heads, q_mine, valid_mine, some(late), earlier=own)
    w_later = swap(after(w_out[cut:], *own), "req", peers, 1)
    w_mine = stage(after(w_out, *own))
    own = attend("attend_own_last", "state", heads, q_mine, valid_mine, some(last), earlier=own)
    attended = combine(own, part, heads)

    have = {0: attended}
    bit = half
    while bit > 1:
        for mask in list(have):
            rows = after(have[mask], have[bit]) if mask else attended
            have[mask ^ bit] = swap(rows, "req", peers, bit)
        bit //= 2

    single = [m for m in have if m and not m & (m - 1)]
    w_later = stage(w_later)
    results, made = {}, []
    for mask in sorted(have, key=lambda m: (m not in single + [0], -m)):
        if mask in single + [0]:
            rows = after(have[mask], *[have[m] for m in single])
        else:
            rows = after(have[mask], *made)
        away, keep = project(rows, w_mine, w_sooner, w_later, cores)
        made += [away, keep]
        away = swap(away, "head", cores, 1)
        summed = (keep + away.astype(jnp.float32)).astype(jnp.bfloat16)
        results[mask] = swap(summed, "req", peers, mask) if mask else summed
    return place(list(results.values()), list(results))


def solution(mesh):
    return jax.shard_map(
        local,
        mesh=mesh,
        in_specs=(
            P(("groups", "req"), "head", None),
            P(("groups", "req"), "head", None),
            P(("groups", "req"), "head", None),
            P(("groups", "req"), "head", None, None, None),
            P("groups"),
            P("groups", None),
            P("groups", "head", None),
            P("head", "req"),
        ),
        out_specs=P(("groups", "req", "head"), None),
        check_vma=False,
    )
```

```python
import functools
import math

import jax
import jax.numpy as jnp
from jax import lax
from jax.experimental import pallas as pl
from jax.experimental.pallas import tpu as pltpu
from jax.sharding import PartitionSpec as P

LOW = -1e30
VMEM_SMALL = 16 * 1024 * 1024
VMEM_MOST = 60 * 1024 * 1024
COST = pl.CostEstimate(flops=1024, bytes_accessed=1024, transcendentals=0)
SHORT = pl.CostEstimate(flops=1 << 31, bytes_accessed=1024, transcendentals=0)
LONG = pl.CostEstimate(flops=1 << 40, bytes_accessed=1024, transcendentals=0)


def swap(array, axis, size, mask):
    return lax.ppermute(array, axis, [(i, i ^ mask) for i in range(size)])


def pack_kernel(wanted, per_peer, slot_ref, ids_ref, kv_ref, *rest):
    outs, (slots, ids, table, sems, first) = rest[:-5], rest[-5:]
    loads = [
        pltpu.make_async_copy(slot_ref, slots, first.at[0]),
        pltpu.make_async_copy(ids_ref, ids, first.at[1]),
    ]
    for copy in loads:
        copy.start()
    for copy in loads:
        copy.wait()
    me = lax.axis_index("req")
    pieces = slots.shape[1]
    held = kv_ref.shape[0]
    picks = ids.shape[0]
    low = me * held
    chosen = [ids[s, me ^ mask] for mask in wanted for s in range(picks)]

    def scan(p, counts):
        later = []
        for row, (c, count) in enumerate(zip(chosen, counts)):
            slot = slots[c, p] - low
            table[row, count] = slot
            later.append(count + ((slot >= 0) & (slot < held)).astype(jnp.int32))
        return tuple(later)

    lax.fori_loop(0, pieces, scan, (jnp.int32(0),) * len(chosen), unroll=4)
    copies = []
    for row in range(len(chosen)):
        out, s = outs[row // picks], row % picks
        for k in range(per_peer):
            copies.append(
                pltpu.make_async_copy(kv_ref.at[table[row, k], 0], out.at[s * per_peer + k], sems.at[len(copies)])
            )
            copies[-1].start()
    for copy in copies:
        copy.wait()


def pack(piece_slot, plan, cluster_kv, wanted, per_peer):
    count = plan.shape[0] * per_peer
    shape = jax.ShapeDtypeStruct((count,) + cluster_kv.shape[2:], cluster_kv.dtype)
    hbm = pl.BlockSpec(memory_space=pltpu.HBM)
    total = len(wanted)
    return pl.pallas_call(
        functools.partial(pack_kernel, wanted, per_peer),
        out_shape=[shape] * total,
        in_specs=[hbm] * 3,
        out_specs=[pl.BlockSpec(memory_space=pltpu.VMEM)] * total,
        scratch_shapes=[
            pltpu.SMEM(piece_slot.shape, jnp.int32),
            pltpu.SMEM(plan.shape, jnp.int32),
            pltpu.SMEM((total * plan.shape[0], per_peer + 1), jnp.int32),
            pltpu.SemaphoreType.DMA((total * count,)),
            pltpu.SemaphoreType.DMA((2,)),
        ],
        compiler_params=pltpu.CompilerParams(vmem_limit_bytes=VMEM_MOST),
        cost_estimate=COST,
        name="pack_pieces",
    )(piece_slot, plan, cluster_kv)


def fold(values, keys, op):
    parts = [values[:, i * keys : (i + 1) * keys] for i in range(values.shape[1] // keys)]
    while len(parts) > 1:
        parts = [op(parts[i], parts[i + 1]) if i + 1 < len(parts) else parts[i] for i in range(0, len(parts), 2)]
    return parts[0]


def to_lines(column, eye):
    keys = eye.shape[0]
    return jnp.concatenate(
        [
            jnp.sum(jnp.where(eye, column[n : n + keys], 0.0), axis=0, keepdims=True)
            for n in range(0, column.shape[0], keys)
        ],
        axis=0,
    )


def to_column(lines, eye):
    return jnp.concatenate(
        [jnp.sum(jnp.where(eye, lines[n : n + 1], 0.0), axis=1, keepdims=True) for n in range(lines.shape[0])],
        axis=0,
    )


def diagonal(keys):
    return lax.broadcasted_iota(jnp.int32, (keys, keys), 0) == lax.broadcasted_iota(jnp.int32, (keys, keys), 1)


def attend_kernel(settings, *refs):
    own, heads, rows_step, sources, scale, mode, earlier = settings
    refs = list(refs)

    def take(n):
        taken, refs[:] = refs[:n], refs[n:]
        return taken

    q_ref, valid_ref = take(2)
    own_k, own_v = take(2) if own else (None, None)
    got = take(len(sources))
    before = take(2) if earlier else None
    outs = take(2)
    scores, own_scores, tops, lse = refs
    rows, size = q_ref.shape
    each, _, keys, _ = got[0].shape
    lines = rows // keys
    group = rows_step // keys
    steps = rows // rows_step
    lane = lax.broadcasted_iota(jnp.int32, (1, keys), 1)
    eye = diagonal(keys)
    biases, any_valid = [], jnp.int32(0)
    for j in sources:
        valid = [valid_ref[j, e] for e in range(each)]
        biases.append(jnp.concatenate([jnp.where(lane < v, 0.0, LOW) for v in valid], axis=1))
        any_valid = sum(valid, any_valid)

    def dot_t(x, y):
        return lax.dot_general(x, y, (((1,), (1,)), ((), ())), preferred_element_type=jnp.float32)

    def score(i, turn):
        q = q_ref[pl.ds(pl.multiple_of(i * rows_step, rows_step), rows_step), :]
        found = []
        if own:
            s = dot_t(q, own_k[...])
            position = (lax.broadcasted_iota(jnp.int32, s.shape, 0) + i * rows_step) // heads
            s = jnp.where(position >= lax.broadcasted_iota(jnp.int32, s.shape, 1), s * scale, LOW)
            own_scores[turn] = s
            found.append(s)
        for b, pieces in enumerate(got):
            s = dot_t(q, pieces[:, 0].reshape(each * keys, size)) * scale + biases[b]
            scores[turn, b] = s
            found.append(fold(s, keys, jnp.maximum))
        tops[turn] = functools.reduce(jnp.maximum, found)

    def weigh(i, turn):
        here = pl.ds(pl.multiple_of(i * rows_step, rows_step), rows_step)
        top = jnp.max(tops[turn], axis=1, keepdims=True)
        total, mix = [], []
        if own:
            p = jnp.exp2(own_scores[turn] - top)
            total.append(fold(p, keys, jnp.add))
            mix.append(jnp.dot(p.astype(jnp.bfloat16), own_v[...], preferred_element_type=jnp.float32))
        for b, pieces in enumerate(got):
            p = jnp.exp2(scores[turn, b] - top)
            total.append(fold(p, keys, jnp.add))
            values = pieces[:, 1].reshape(each * keys, size)
            mix.append(jnp.dot(p.astype(jnp.bfloat16), values, preferred_element_type=jnp.float32))
        total = jnp.sum(functools.reduce(jnp.add, total), axis=1, keepdims=True)
        normal = functools.reduce(jnp.add, mix) / total
        mine = to_lines(top + jnp.log2(total), eye)
        if not own:
            mine = jnp.where(any_valid > 0, mine, LOW)
        if earlier:
            old, logs = before[0][here, :], before[1][i]
            peak = jnp.maximum(logs, mine)
            power = jnp.exp2(logs - peak)
            whole = power + jnp.exp2(mine - peak)
            normal = normal + to_column(power / whole, eye) * (old - normal)
            mine = peak + jnp.log2(whole)
        if mode == "state":
            outs[0][here, :] = normal
            outs[1][i] = mine
        else:
            lse[i] = mine
            low = normal.astype(jnp.bfloat16)
            for n in range(2):

                @pl.when(i // (steps // 2) == n)
                def _(n=n):
                    spot = pl.multiple_of((i - n * (steps // 2)) * rows_step, rows_step)
                    outs[n][pl.ds(spot, rows_step), :] = low

    score(0, 0)

    def each_step(i, carry):
        for turn in range(2):
            score(jnp.minimum(2 * i + turn + 1, steps - 1), 1 - turn)
            weigh(2 * i + turn, turn)
        return carry

    lax.fori_loop(0, steps // 2, each_step, 0)
    if mode == "packed":
        left = jnp.concatenate([lse[i] for i in range(steps)], axis=0)
        for n in range(3):
            part = left.astype(jnp.bfloat16)
            outs[0][pl.ds(rows // 2 + n * lines, lines), :] = part
            left = left - part.astype(jnp.float32)


def attend(name, mode, heads, q, valid, got, own=None, earlier=None, cost=COST):
    rows, size = q.shape
    sources = list(got)
    each, _, keys, _ = got[sources[0]].shape
    rows_step = math.gcd(rows, 512)
    lines = rows // keys
    scale = size ** -0.5 * math.log2(math.e)
    settings = (own is not None, heads, rows_step, sources, scale, mode, earlier is not None)
    smem = pl.BlockSpec(memory_space=pltpu.SMEM)
    vmem = pl.BlockSpec(memory_space=pltpu.VMEM)
    operands = [q, valid] + list(own or ()) + list(got.values()) + list(earlier or ())
    if mode == "state":
        out_shape = [
            jax.ShapeDtypeStruct((rows, size), jnp.float32),
            jax.ShapeDtypeStruct((rows // rows_step, rows_step // keys, keys), jnp.float32),
        ]
    else:
        out_shape = [jax.ShapeDtypeStruct((n, size), jnp.bfloat16) for n in (rows // 2 + 3 * lines, rows // 2)]
    limit = min(VMEM_MOST, VMEM_SMALL + 8 * len(sources) * rows_step * each * keys)
    return pl.pallas_call(
        functools.partial(attend_kernel, settings),
        out_shape=out_shape,
        in_specs=[vmem, smem] + [vmem] * (len(operands) - 2),
        out_specs=[vmem] * len(out_shape),
        scratch_shapes=[
            pltpu.VMEM((2, len(sources), rows_step, each * keys), jnp.float32),
            pltpu.VMEM((2, rows_step if own is not None else 8, own[0].shape[0] if own else keys), jnp.float32),
            pltpu.VMEM((2, rows_step, keys), jnp.float32),
            pltpu.VMEM((rows // rows_step, rows_step // keys, keys), jnp.float32),
        ],
        compiler_params=pltpu.CompilerParams(vmem_limit_bytes=limit),
        cost_estimate=cost,
        name=name,
    )(*operands)


def combine_kernel(heads, out_mine, lse_mine, other, more, attended, scratch):
    rows, size = out_mine.shape
    steps, group, keys = lse_mine.shape
    lines = steps * group
    eye = diagonal(keys)
    mine = jnp.concatenate([lse_mine[i] for i in range(steps)], axis=0)
    theirs = sum(other[pl.ds(rows // 2 + n * lines, lines), :].astype(jnp.float32) for n in range(3))
    top = jnp.maximum(mine, theirs)
    mine, theirs = jnp.exp2(mine - top), jnp.exp2(theirs - top)
    share = theirs / (mine + theirs)
    for n in range(lines):
        here = pl.ds(n * keys, keys)
        a = out_mine[here, :]
        b = other[here, :] if n < lines // 2 else more[pl.ds((n - lines // 2) * keys, keys), :]
        scratch[here, :] = a + to_column(share[n : n + 1], eye) * (b.astype(jnp.float32) - a)
    tokens = rows // heads
    for h in range(heads):
        attended[:, h * size : (h + 1) * size] = scratch[pl.ds(h, tokens, stride=heads), :].astype(attended.dtype)


def combine(state, parts, heads):
    rows, size = state[0].shape
    vmem = pl.BlockSpec(memory_space=pltpu.VMEM)
    return pl.pallas_call(
        functools.partial(combine_kernel, heads),
        out_shape=jax.ShapeDtypeStruct((rows // heads, heads * size), jnp.bfloat16),
        in_specs=[vmem] * 4,
        out_specs=vmem,
        scratch_shapes=[pltpu.VMEM((rows, size), jnp.float32)],
        compiler_params=pltpu.CompilerParams(vmem_limit_bytes=VMEM_SMALL),
        cost_estimate=LONG,
        name="combine",
    )(*state, *parts)


def stage_kernel(source, target, sems):
    rows = source.shape[0] // sems.shape[0]
    copies = []
    for n in range(sems.shape[0]):
        part = pl.ds(n * rows, rows)
        copies.append(pltpu.make_async_copy(source.at[part], target.at[part], sems.at[n]))
        copies[-1].start()
    for copy in copies:
        copy.wait()


def stage(array):
    return pl.pallas_call(
        stage_kernel,
        out_shape=jax.ShapeDtypeStruct(array.shape, array.dtype),
        in_specs=[pl.BlockSpec(memory_space=pl.ANY)],
        out_specs=pl.BlockSpec(memory_space=pltpu.VMEM),
        scratch_shapes=[pltpu.SemaphoreType.DMA((8,))],
        compiler_params=pltpu.CompilerParams(vmem_limit_bytes=VMEM_SMALL),
        cost_estimate=COST,
        name="stage",
    )(array)


def project_kernel(attended, w_mine, w_sooner, w_later, away, keep, scratch):
    core = lax.axis_index("head")
    share = away.shape[1]
    cut = w_sooner.shape[0]

    def dot(x, w):
        return jnp.dot(x, w[...], preferred_element_type=jnp.float32)

    scratch[0] = dot(attended[...], w_mine)
    scratch[1] = dot(attended[:, :cut], w_sooner) + dot(attended[:, cut:], w_later)
    for side in range(2):
        away[side] = scratch[side, pl.ds(pl.multiple_of((core ^ 1) * share, share), share), :].astype(jnp.bfloat16)
        keep[side] = scratch[side, pl.ds(pl.multiple_of(core * share, share), share), :]


def project(attended, w_mine, w_sooner, w_later, cores):
    tokens, depth = attended.shape
    width = w_mine.shape[1]
    share = tokens // cores
    vmem = pl.BlockSpec(memory_space=pltpu.VMEM)
    return pl.pallas_call(
        project_kernel,
        out_shape=[
            jax.ShapeDtypeStruct((2, share, width), jnp.bfloat16),
            jax.ShapeDtypeStruct((2, share, width), jnp.float32),
        ],
        in_specs=[vmem] * 4,
        out_specs=[vmem] * 2,
        scratch_shapes=[pltpu.VMEM((2, tokens, width), jnp.float32)],
        compiler_params=pltpu.CompilerParams(vmem_limit_bytes=VMEM_SMALL),
        cost_estimate=COST,
        name="project",
    )(attended, w_mine, w_sooner, w_later)


def place_kernel(masks, *refs):
    parts, out = refs[:-1], refs[-1]
    me = lax.axis_index("req")
    width = parts[0].shape[2]
    for part, mask in zip(parts, masks):
        for side in range(2):
            column = ((me ^ mask) ^ side) * width
            out[:, pl.ds(pl.multiple_of(column, width), width)] = part[side]


def place(parts, masks):
    _, rows, width = parts[0].shape
    vmem = pl.BlockSpec(memory_space=pltpu.VMEM)
    return pl.pallas_call(
        functools.partial(place_kernel, masks),
        out_shape=jax.ShapeDtypeStruct((rows, 2 * len(parts) * width), parts[0].dtype),
        in_specs=[vmem] * len(parts),
        out_specs=vmem,
        compiler_params=pltpu.CompilerParams(vmem_limit_bytes=VMEM_SMALL),
        cost_estimate=COST,
        name="place_columns",
    )(*parts)


def after(value, *others):
    return lax.optimization_barrier((value, others))[0]


def local(queries, new_keys, new_values, cluster_kv, cluster_len, piece_slot, cluster_ids, w_out):
    me = lax.axis_index("req")
    peers = lax.axis_size("req")
    cores = lax.axis_size("head")
    tokens, heads, size = queries.shape
    held = cluster_kv.shape[0]
    keys = cluster_kv.shape[3]
    pieces = piece_slot.shape[1]
    per_peer = pieces // peers
    half = peers // 2
    masks = list(range(1, half))
    last, late, early = masks[-1:], masks[-2:-1], masks[:-2]

    plan = cluster_ids[:, 0]
    first = pack(piece_slot, plan.T, cluster_kv, [m ^ half for m in masks], per_peer)
    got = {m: swap(a, "req", peers, m) for a, m in zip(first, masks)}
    q_mine = queries.reshape(tokens * heads, size)
    q_theirs = swap(q_mine, "req", peers, half)
    second = pack(piece_slot, plan.T, after(cluster_kv, *first), [half, 0] + masks, per_peer)
    got[0], own_pieces, second = second[0], second[1], dict(zip(masks, second[2:]))

    owner = piece_slot // held
    position = jnp.arange(pieces, dtype=jnp.int32)
    same = (owner[:, :, None] == owner[:, None, :]) & (position[:, None] > position[None, :])[None]
    rank = jnp.sum(same.astype(jnp.int32), axis=2)

    def table(request):
        chosen = lax.dynamic_index_in_dim(plan, request, 0, keepdims=False)
        sender = me ^ jnp.arange(half, dtype=jnp.int32)
        fits = (owner[chosen][None, :, None, :] == sender[:, None, None, None]) & (
            rank[chosen][None, :, None, :] == jnp.arange(per_peer, dtype=jnp.int32)[None, None, :, None]
        )
        filled = jnp.clip(cluster_len[chosen][:, None] - position[None, :] * keys, 0, keys)
        return jnp.sum(jnp.where(fits, filled[None, :, None, :], 0), axis=3).reshape(half, -1)

    valid_theirs, valid_mine = table(me ^ half), table(me)

    def some(chosen):
        return {m: got[m] for m in chosen}

    own = attend(
        "attend_own_local", "state", heads, after(q_mine, valid_theirs, got[0]), valid_mine, {0: own_pieces},
        (new_keys[:, 0], new_values[:, 0]),
    )
    q_theirs = after(q_theirs, *own)
    state = attend("attend_partner_local", "state", heads, q_theirs, valid_theirs, some([0]), cost=SHORT)
    if early:
        state = attend("attend_partner_early", "state", heads, q_theirs, valid_theirs, some(early), earlier=state)
    got_mine = {m: swap(after(second[m], *state), "req", peers, m) for m in masks}
    state = attend("attend_partner_late", "state", heads, q_theirs, valid_theirs, some(late), earlier=state)
    part = attend("attend_partner_last", "packed", heads, q_theirs, valid_theirs, some(last), earlier=state)
    got = got_mine
    cut = w_out.shape[0] * 3 // 16
    w_sooner = swap(after(w_out[:cut], *part), "req", peers, 1)
    own = after(own, *part)
    part = [swap(a, "req", peers, half) for a in part]

    if early:
        own = attend("attend_own_early", "state", heads, q_mine, valid_mine, some(early), earlier=own)
    own = after(own, w_sooner)
    own = attend("attend_own_late", "state", heads, q_mine, valid_mine, some(late), earlier=own)
    w_later = swap(after(w_out[cut:], *own), "req", peers, 1)
    w_mine = stage(after(w_out, *own))
    own = attend("attend_own_last", "state", heads, q_mine, valid_mine, some(last), earlier=own)
    attended = combine(own, part, heads)

    have = {0: attended}
    bit = half
    while bit > 1:
        for mask in list(have):
            rows = after(have[mask], have[bit]) if mask else attended
            have[mask ^ bit] = swap(rows, "req", peers, bit)
        bit //= 2

    single = [m for m in have if m and not m & (m - 1)]
    w_later = stage(w_later)
    results, made = {}, []
    for mask in sorted(have, key=lambda m: (m not in single + [0], -m)):
        if mask in single + [0]:
            rows = after(have[mask], *[have[m] for m in single])
        else:
            rows = after(have[mask], *made)
        away, keep = project(rows, w_mine, w_sooner, w_later, cores)
        made += [away, keep]
        away = swap(away, "head", cores, 1)
        summed = (keep + away.astype(jnp.float32)).astype(jnp.bfloat16)
        results[mask] = swap(summed, "req", peers, mask) if mask else summed
    return place(list(results.values()), list(results))


def solution(mesh):
    return jax.shard_map(
        local,
        mesh=mesh,
        in_specs=(
            P(("groups", "req"), "head", None),
            P(("groups", "req"), "head", None),
            P(("groups", "req"), "head", None),
            P(("groups", "req"), "head", None, None, None),
            P("groups"),
            P("groups", None),
            P("groups", "head", None),
            P("head", "req"),
        ),
        out_specs=P(("groups", "req", "head"), None),
        check_vma=False,
    )
```
